512 devices in a mesh: member: 8 (over y_lo, core), patch: 64 (over x, y_hi, z).
Axes of the slice: x: 4, y: 8 (y_hi: 2, y_lo: 4; y = y_hi * 4 + y_lo), z: 8, core: 2. Of those that a mesh axis runs over, the one named last changes fastest.
Arguments:
- perturbations: float32 [64, 55, 16384], P('member', None, 'patch'), may hold values from -6 to 6
- gradient: float32 [55, 64, 256], P(None, 'patch', 'member'), may hold values from -6 to 6
- kappa: float32 [16384], P('patch'), may hold values from 0.02 to 0.08
- vloc: float32 [55, 55], replicated, may hold values from -0.875 to 0.875
- neighbors: int32 [6, 16384], P(None, 'patch'), may hold values from 0 to 320, as said below
- send_lists: int32 [4, 1024], P(None, 'patch'), may hold values from 0 to 255, as said below
- counts: int32 [64], P('patch'), may hold values from 248 to 256, as said below
Outputs:
- control_gradient: float32 [64, 55, 16384], P('member', None, 'patch')
The draws below stay inside these ranges and needn't reach their ends.
Inputs may be any that keep to these rules, and one draw needn't show every extreme that they name: `neighbors`: neighbor relations are symmetric; live cells only name live cells; entries at or above 256 name the received cells of the four neighboring patches; cells of slots at or above the patch's count have only empty entries. `send_lists`: each entry is the slot of a live cell of the sending patch. `counts`: some patch is full.
All inputs are finite; a program needn't handle non-finite values.
Results may differ from the reference program's by a relative error of at most 0.000073.
Values sent between devices are 32-bit elements; how exact they have to be, the bound alone decides.
No kernel may reach another device: no remote copies, remote signals or barrier semaphores. Data moves between devices by JAX's collectives and lax.ppermute only.
A program may use at most 64 MiB of HBM per device.

```python
import math
import jax
import jax.numpy as jnp
from jax import lax

LEV = 55
S = 16
PW = 8
STEPS = 4
C = 256
PATCHES = 64
CELLS = 16384
MEMBERS = 64


def mesh_tables(key):
    cell_total = S * S
    key_dead, key_pick, key_slot = jax.random.split(key, 3)
    patch_ids = jnp.arange(PATCHES, dtype=jnp.int32)
    dead_count = jax.random.randint(key_dead, (PATCHES,), 0, S // 2 + 1).astype(jnp.int32)
    dead_count = jnp.where(patch_ids == 0, 0, dead_count)
    dead_count = jnp.where(patch_ids == 1, S // 2, dead_count).astype(jnp.int32)
    positions = jnp.arange(cell_total, dtype=jnp.int32)
    row_index = positions // S
    col_index = positions % S
    interior = (row_index >= 1) & (row_index <= S - 2) & (col_index >= 1) & (col_index <= S - 2)
    pick_rank = jax.vmap(lambda item: jax.random.permutation(item, cell_total))(jax.random.split(key_pick, PATCHES)).astype(jnp.int32)
    score = jnp.where(interior[None, :], pick_rank, cell_total + pick_rank)
    position_rank = jnp.argsort(jnp.argsort(score, axis=1, stable=True), axis=1, stable=True)
    dead_pos = position_rank < dead_count[:, None]
    slot_rank = jax.vmap(lambda item: jax.random.permutation(item, cell_total))(jax.random.split(key_slot, PATCHES)).astype(jnp.int32)
    first_patch = patch_ids[:, None] == 0
    slot_rank = jnp.where(first_patch & (positions[None, :] == 0), 2 * cell_total, slot_rank)
    slot_rank = jnp.where(first_patch & (positions[None, :] == S - 1), -1, slot_rank).astype(jnp.int32)
    slot_order = jnp.argsort(slot_rank + 3 * cell_total * dead_pos.astype(jnp.int32), axis=1, stable=True).astype(jnp.int32)
    slot_of_pos = jnp.argsort(slot_order, axis=1, stable=True).astype(jnp.int32)
    null_index = cell_total + 4 * S
    row_steps = (0, 0, -1, 1, -1, 1)
    col_steps = (-1, 1, 0, 0, 1, -1)
    ghost_first = (cell_total + row_index, cell_total + S + row_index, cell_total + 2 * S + col_index, cell_total + 3 * S + col_index, jnp.full((cell_total,), null_index, jnp.int32), jnp.full((cell_total,), null_index, jnp.int32))
    tables = []
    for column in range(6):
        row_next = row_index + row_steps[column]
        col_next = col_index + col_steps[column]
        inside = (row_next >= 0) & (row_next < S) & (col_next >= 0) & (col_next < S)
        target = jnp.clip(row_next, 0, S - 1) * S + jnp.clip(col_next, 0, S - 1)
        target_all = jnp.broadcast_to(target[None, :], (PATCHES, cell_total))
        local = jnp.take_along_axis(slot_of_pos, target_all, axis=1)
        target_dead = jnp.take_along_axis(dead_pos, target_all, axis=1)
        ghost = jnp.broadcast_to(ghost_first[column][None, :], (PATCHES, cell_total))
        entry = jnp.where(inside[None, :], jnp.where(target_dead, null_index, local), ghost)
        entry = jnp.where(dead_pos, null_index, entry)
        tables.append(jnp.take_along_axis(entry, slot_order, axis=1))
    neighbor_table = jnp.stack(tables, 0).reshape(6, PATCHES * cell_total).astype(jnp.int32)
    line = jnp.arange(S, dtype=jnp.int32)
    block_positions = (line * S + S - 1, line * S, (S - 1) * S + line, line)
    send_table = jnp.stack([slot_of_pos[:, item] for item in block_positions], 0).reshape(4, PATCHES * S).astype(jnp.int32)
    live_counts = (cell_total - dead_count).astype(jnp.int32)
    return (neighbor_table, send_table, live_counts)


def draw_neighbors(key, part):
    tables = mesh_tables(key)
    return tables[0]


def draw_send_lists(key, part):
    tables = mesh_tables(key)
    return tables[1]


def draw_counts(key, part):
    tables = mesh_tables(key)
    return tables[2]


def levels(rng, shape, cuts, low, largest):
    factor_of = 1.0
    for dim, shards_of in cuts:
        draws = jax.random.uniform(jax.random.fold_in(jax.random.fold_in(rng, 6), dim), (shards_of,), jnp.float32, low / len(cuts), largest / len(cuts))
        factor_of = factor_of * jnp.repeat(jnp.exp(draws), shape[dim] // shards_of).reshape((-1,) + (1,) * (len(shape) - 1 - dim))
    return factor_of


def bell_draw(own_key, extent, width, limit, cuts=(), kind=jnp.bfloat16):
    drawn = jax.random.normal(own_key, extent, jnp.float32) * width
    if len(cuts) > 0:
        drawn = levels(own_key, extent, cuts, -0.22, 0.18) * drawn
    return jnp.clip(drawn, min=-limit, max=limit).astype(kind)


def setup_inputs(seed: int = 0) -> dict:
    splits = jax.random.split(jax.random.key(seed), 8)
    perturbations = bell_draw(splits[0], (MEMBERS, LEV, CELLS), 1.0, 6.0, ((0, 8), (2, 64)), jnp.float32)
    gradient = bell_draw(splits[1], (LEV, PATCHES, C), 1.0, 6.0, ((1, 64), (2, 8)), jnp.float32)
    kappa = jnp.clip(jnp.exp(math.log(0.08) - 1.3862944 * jax.random.uniform(splits[2], (CELLS,), jnp.float32) ** levels(splits[2], (CELLS,), ((0, 64),), -0.2, 0.2)), 0.02, 0.08)
    vloc = bell_draw(splits[3], (LEV, LEV), LEV ** -0.5, 0.875, (), jnp.float32)
    neighbors = draw_neighbors(jax.random.fold_in(splits[7], 71), 0)
    send_lists = draw_send_lists(jax.random.fold_in(splits[7], 71), 0)
    counts = draw_counts(jax.random.fold_in(splits[7], 71), 0)
    return {"perturbations": perturbations, "gradient": gradient, "kappa": kappa, "vloc": vloc, "neighbors": neighbors, "send_lists": send_lists, "counts": counts}


def reference(perturbations, gradient, kappa, vloc, neighbors, send_lists, counts):
    cell_total = S * S
    cell_count = cell_total * PATCHES
    patch_of = (jnp.arange(cell_count) // cell_total).astype(jnp.int32)
    slot_of = (jnp.arange(cell_count) % cell_total).astype(jnp.int32)
    ghost_block = jnp.clip((neighbors - cell_total) // S, 0, 3).astype(jnp.int32)
    within = ((neighbors - cell_total) % S).astype(jnp.int32)
    offsets = jnp.array([1, -1, PW, -PW], jnp.int32)
    source = (patch_of[None, :] - offsets[ghost_block]) % PATCHES
    ghost_global = source * cell_total + send_lists[ghost_block, source * S + within]
    global_index = jnp.where(neighbors < cell_total, patch_of[None, :] * cell_total + neighbors,
                             jnp.where(neighbors < cell_total + 4 * S, ghost_global, cell_count)).astype(jnp.int32)
    degree = jnp.sum((neighbors < cell_total + 4 * S).astype(jnp.float32), axis=0)
    field_gradient = gradient.reshape(LEV, cell_count)
    alive_mask = (slot_of < counts[patch_of]).astype(jnp.float32)

    def one_member(member_field):
        state = member_field * field_gradient
        for step in range(STEPS):
            flux = kappa[None, :] * state
            padded = jnp.concatenate([flux, jnp.zeros((LEV, 1), flux.dtype)], axis=1)
            total = padded[:, global_index[0]]
            for column in range(1, 6):
                total = total + padded[:, global_index[column]]
            state = state - degree[None, :] * flux + total
        mixed = jnp.dot(vloc.T, state, precision=lax.Precision.HIGHEST)
        return mixed * alive_mask[None, :]

    return lax.map(one_member, perturbations)
```

```python
import itertools

import jax
import jax.numpy as jnp
from jax import lax
from jax.experimental import pallas as pl
from jax.experimental.pallas import tpu as pltpu
from jax.sharding import Mesh
from jax.sharding import PartitionSpec as P

STEPS = 4
AXES = ("member", "x", "yh", "z")
LEV = 55
ROWS = 56
MEM = 8
FIELDS = MEM * ROWS
CELLS = 256
RIM = 16
GHOSTS = 4 * RIM
NULL = CELLS + GHOSTS
SLOT = 24
F32 = jnp.float32
BF16 = jnp.bfloat16


def flat(x, yh, l, z, core):
    return (l * 2 + core) * 64 + (x % 4) * 16 + yh * 8 + z % 8


def pairs(move):
    every = itertools.product(range(4), range(2), range(4), range(8), range(2))
    return sorted((flat(*c), flat(*move(*c))) for c in every)


def next_column(x, yh, l, z, core):
    if z < 7:
        return x, yh, l, z + 1, core
    return x + core, yh, l, 0, 1 - core


SWAP = pairs(lambda x, yh, l, z, core: (x, core, l, z, yh))
EAST = pairs(next_column)
WEST = sorted((b, a) for a, b in EAST)
SOUTH = pairs(lambda x, yh, l, z, core: (x + core, yh, l, z, 1 - core))
NORTH = sorted((b, a) for a, b in SOUTH)
ROUTES = (EAST, WEST, SOUTH, NORTH)
ORDER = (0, 2, 1, 3)


def thirds(value):
    high = value.astype(BF16)
    rest = value - high.astype(F32)
    middle = rest.astype(BF16)
    low = (rest - middle.astype(F32)).astype(BF16)
    return high, middle, low


def exact_dot(left, right, dims):
    split_left = left.dtype == F32
    total = None
    for part in reversed(thirds(left if split_left else right)):
        a, b = (part, right) if split_left else (left, part)
        term = lax.dot_general(a, b, (dims, ((), ())), preferred_element_type=F32)
        total = term if total is None else total + term
    return total


def pack_kernel(member, grad, table, out):
    piece = jnp.concatenate([grad[...], jnp.zeros((4 * RIM - LEV, 32), F32)], axis=0)
    out[0, 0:RIM, :] = jnp.concatenate(
        [piece[g * RIM : (g + 1) * RIM] for g in range(4)], axis=1
    )
    row = table[pl.ds(member[0], 1), :]
    out[0, RIM:, :] = jnp.concatenate(
        [row[:, :128], row[:, 128:], jnp.zeros((SLOT - RIM - 2, 128), F32)], axis=0
    )
    for s in range(1, 16):
        out[s] = out[0]


def rims_out(rims, outs):
    for d in range(4):
        outs[d][...] = rims[d * RIM : (d + 1) * RIM]


def first_kernel(core, slots, pert, r0, r1, r2, r3, x_out, adj_out, sel_out, rows_out):
    base = core[0] * MEM
    lane = lax.broadcasted_iota(jnp.int32, (RIM, 128), 1)
    halves = [[], []]
    for g in range(4):
        for half in range(2):
            total = jnp.zeros((RIM, 128), F32)
            for i in range(4):
                piece = slots[base + half * 4 + i, 0:RIM, :]
                shift = (32 * (i - g)) % 128
                moved = pltpu.roll(piece, shift, 1) if shift else piece
                total = jnp.where(lane // 32 == i, moved, total)
            halves[half].append(total)
    grad = jnp.concatenate(
        [jnp.concatenate(halves[0], axis=0), jnp.concatenate(halves[1], axis=0)], axis=1
    )

    def table_row(j):
        two = slots[base + j, RIM : RIM + 8, :]
        return jnp.concatenate([two[0:1], two[1:2]], axis=1)

    kappa = table_row(6)
    misc = table_row(7)
    ids = lax.broadcasted_iota(jnp.int32, (NULL, CELLS), 0)
    adj = jnp.zeros((NULL, CELLS), F32)
    degree = jnp.zeros((1, CELLS), F32)
    for j in range(6):
        named = table_row(j).astype(jnp.int32)
        adj = adj + (ids == named).astype(F32)
        degree = degree + (named < NULL).astype(F32)
    adj_out[...] = adj.astype(BF16)
    sends = jnp.broadcast_to(misc[:, :128], (128, 128)).T
    sends = jnp.concatenate([sends[0:GHOSTS], sends[0:GHOSTS]], axis=1).astype(jnp.int32)
    sel = (sends == lax.broadcasted_iota(jnp.int32, (GHOSTS, CELLS), 1)).astype(F32)
    sel = sel.astype(BF16)
    sel_out[...] = sel
    count = jnp.max(
        jnp.where(lax.broadcasted_iota(jnp.int32, (1, 128), 1) == GHOSTS, misc[:, :128], 0.0),
        axis=1,
        keepdims=True,
    ).astype(jnp.int32)
    alive = (lax.broadcasted_iota(jnp.int32, (1, CELLS), 1) < count).astype(F32)
    rows_out[...] = jnp.concatenate(
        [kappa, 1.0 - degree * kappa, alive, jnp.zeros((5, CELLS), F32)], axis=0
    )
    for m in range(MEM):
        x_out[m * ROWS : m * ROWS + LEV, :] = pert[m] * grad[0:LEV]
        x_out[m * ROWS + LEV : (m + 1) * ROWS, :] = jnp.zeros((1, CELLS), F32)
    rims = exact_dot(sel, kappa * x_out[...], ((1,), (1,)))
    rims_out(rims, (r0, r1, r2, r3))


def stay(x, adj, sel, rows, y_out, b_out):
    kappa = rows[0:1, :]
    y = x * rows[1:2, :] + exact_dot(kappa * x, adj[0:CELLS, :], ((1,), (0,)))
    y_out[...] = y
    if b_out is not None:
        b_out[...] = exact_dot(sel[...], kappa * y, ((1,), (1,)))


def first_stay_kernel(x, adj, sel, rows, y_out, b_out, gsel_out, ksel_out):
    stay(x[...], adj, sel, rows, y_out, b_out)
    gsel_out[...] = lax.dot_general(
        sel[...], adj[CELLS:, :], (((1,), (1,)), ((), ())), preferred_element_type=F32
    ).astype(BF16)
    ksel_out[...] = exact_dot(
        sel[...], jnp.broadcast_to(rows[0:1, :], (128, CELLS)), ((1,), (1,))
    )


def rim_kernel(b, gsel, ksel, i0, i1, i2, i3, r0, r1, r2, r3):
    came = jnp.concatenate([i0[...], i1[...], i2[...], i3[...]], axis=0)
    rims = b[...] + ksel[:, 0:1] * exact_dot(gsel[...], came, ((1,), (0,)))
    rims_out(rims, (r0, r1, r2, r3))


def arrive(y, adj, i0, i1, i2, i3):
    came = jnp.concatenate([i0[...], i1[...], i2[...], i3[...]], axis=0)
    return y[...] + exact_dot(came.T, adj[CELLS:, :], ((1,), (0,)))


def stay_kernel(y, adj, sel, rows, i0, i1, i2, i3, y_out, b_out=None):
    stay(arrive(y, adj, i0, i1, i2, i3), adj, sel, rows, y_out, b_out)


def last_kernel(y, adj, rows, vloc, i0, i1, i2, i3, out):
    x = arrive(y, adj, i0, i1, i2, i3)
    mix = vloc[...].T
    for m in range(MEM):
        part = x[m * ROWS : m * ROWS + LEV] * rows[2:3, :]
        out[m] = jnp.dot(
            mix, part, precision=lax.Precision.HIGHEST, preferred_element_type=F32
        )


VM = pl.BlockSpec(memory_space=pltpu.VMEM)
SM = pl.BlockSpec(memory_space=pltpu.SMEM)


def call(kernel, shapes, args, scalars=0, flops=10**8):
    specs = [SM] * scalars + [VM] * (len(args) - scalars)
    return pl.pallas_call(
        kernel,
        out_shape=[jax.ShapeDtypeStruct(s, t) for s, t in shapes],
        in_specs=specs,
        out_specs=[VM] * len(shapes),
        cost_estimate=pl.CostEstimate(flops=flops, bytes_accessed=10**6, transcendentals=0),
        compiler_params=pltpu.CompilerParams(vmem_limit_bytes=32 * 1024 * 1024),
    )(*args)


def exchange(rims):
    came = {d: lax.ppermute(rims[d], AXES, ROUTES[d]) for d in ORDER}
    return [came[d] for d in range(4)]


def local(perturbations, gradient, kappa, vloc, neighbors, send_lists, counts):
    pert = lax.ppermute(perturbations, AXES, SWAP)
    member = lax.axis_index("member")
    misc = jnp.concatenate(
        [
            send_lists.reshape(GHOSTS),
            counts.reshape(1),
            jnp.zeros((CELLS - GHOSTS - 1,), jnp.int32),
        ]
    )
    table = jnp.concatenate(
        [neighbors.astype(F32), kappa.reshape(1, CELLS), misc.reshape(1, CELLS).astype(F32)]
    )
    (slots,) = call(
        pack_kernel,
        [((16, SLOT, 128), F32)],
        (member.reshape(1), gradient.reshape(LEV, 32), table),
        scalars=1,
    )
    slots = lax.all_to_all(slots, ("yh", "member"), 0, 0)
    rim_shapes = [((RIM, FIELDS), F32)] * 4
    state = ((FIELDS, CELLS), F32)
    border = ((GHOSTS, FIELDS), F32)
    *rims, x, adj, sel, rows = call(
        first_kernel,
        rim_shapes
        + [state, ((NULL, CELLS), BF16), ((GHOSTS, CELLS), BF16), ((8, CELLS), F32)],
        ((member % 2).reshape(1), slots, pert),
        scalars=1,
    )
    came = exchange(rims)
    y, b, gsel, ksel = call(
        first_stay_kernel,
        [state, border, ((GHOSTS, GHOSTS), BF16), ((GHOSTS, 128), F32)],
        (x, adj, sel, rows),
    )
    for step in range(1, STEPS):
        rims = call(rim_kernel, rim_shapes, (b, gsel, ksel, *came))
        shapes = [state, border] if step < STEPS - 1 else [state]
        y, *b = call(stay_kernel, shapes, (y, adj, sel, rows, *came))
        b = b[0] if b else None
        came = exchange(rims)
    (out,) = call(
        last_kernel, [((MEM, LEV, CELLS), F32)], (y, adj, rows, vloc, *came)
    )
    return lax.ppermute(out, AXES, SWAP)


def solution(mesh):
    near = Mesh(mesh.devices.reshape(8, 4, 2, 8), AXES)
    patch = ("x", "yh", "z")
    return jax.shard_map(
        local,
        mesh=near,
        in_specs=(
            P("member", None, patch),
            P(None, patch, "member"),
            P(patch),
            P(),
            P(None, patch),
            P(None, patch),
            P(patch),
        ),
        out_specs=P("member", None, patch),
        check_vma=False,
    )
```

```python
import itertools

import jax
import jax.numpy as jnp
from jax import lax
from jax.experimental import pallas as pl
from jax.experimental.pallas import tpu as pltpu
from jax.sharding import Mesh
from jax.sharding import PartitionSpec as P

STEPS = 4
AXES = ("member", "x", "yh", "z")
LEV = 55
MEM = 8
FIELDS = LEV * MEM
CELLS = 256
RIM = 16
GHOSTS = 4 * RIM
NULL = CELLS + GHOSTS
SLOT = 24
F32 = jnp.float32
BF16 = jnp.bfloat16


def flat(x, yh, l, z, core):
    return (l * 2 + core) * 64 + (x % 4) * 16 + yh * 8 + z % 8


def pairs(move):
    every = itertools.product(range(4), range(2), range(4), range(8), range(2))
    return sorted((flat(*c), flat(*move(*c))) for c in every)


def next_column(x, yh, l, z, core):
    if z < 7:
        return x, yh, l, z + 1, core
    return x + core, yh, l, 0, 1 - core


SWAP = pairs(lambda x, yh, l, z, core: (x, core, l, z, yh))
EAST = pairs(next_column)
WEST = sorted((b, a) for a, b in EAST)
SOUTH = pairs(lambda x, yh, l, z, core: (x + core, yh, l, z, 1 - core))
NORTH = sorted((b, a) for a, b in SOUTH)
ROUTES = (EAST, SOUTH, WEST, NORTH)
ORDER = (0, 2, 1, 3)


def thirds(value):
    high = value.astype(BF16)
    rest = value - high.astype(F32)
    middle = rest.astype(BF16)
    low = (rest - middle.astype(F32)).astype(BF16)
    return high, middle, low


def exact_dot(left, right, dims):
    split_left = left.dtype == F32
    total = None
    for part in reversed(thirds(left if split_left else right)):
        a, b = (part, right) if split_left else (left, part)
        term = lax.dot_general(a, b, (dims, ((), ())), preferred_element_type=F32)
        total = term if total is None else total + term
    return total


def pack_kernel(member, count, grad, kappa, named, sends, out, table):
    table[0:6, :] = named[...].astype(F32)
    table[6:7, :] = kappa[...]
    row = [sends[d : d + 1, :].astype(F32) for d in range(4)]
    row.append(jnp.full((1, 128 - GHOSTS), count[0].astype(F32)))
    table[7:8, 0:128] = jnp.concatenate(row, axis=1)
    table[7:8, 128:] = jnp.zeros((1, 128), F32)
    piece = jnp.concatenate([grad[...], jnp.zeros((32, 64 - LEV), F32)], axis=1)
    out[0, 0:RIM, :] = jnp.concatenate([piece[0:RIM], piece[RIM:]], axis=1)
    row = table[pl.ds(member[0], 1), :]
    out[0, RIM:, :] = jnp.concatenate(
        [row[:, :128], row[:, 128:], jnp.zeros((SLOT - RIM - 2, 128), F32)], axis=0
    )
    for s in range(1, 16):
        out[s] = out[0]


def rims_out(rims, outs):
    for d, out in zip(ORDER, outs):
        out[...] = rims[d * RIM : (d + 1) * RIM]


def joined(arrived):
    return jnp.concatenate([arrived[d][...] for d in ORDER], axis=0)


def first_kernel(core, slots, pert, r0, r1, r2, r3, x_out, adj_out, sel_out, rows_out):
    base = core[0] * MEM
    cells = []
    for m in range(MEM):
        two = slots[base + m, 0:RIM, :]
        cells += [two, pltpu.roll(two, 64, 1)]
    grad = jnp.concatenate(cells, axis=0).T

    def table_row(j):
        two = slots[base + j, RIM : RIM + 8, :]
        return jnp.concatenate([two[0:1], two[1:2]], axis=1)

    kappa = table_row(6)
    misc = table_row(7)
    ids = lax.broadcasted_iota(jnp.int32, (NULL, CELLS), 0)
    adj = jnp.zeros((NULL, CELLS), F32)
    degree = jnp.zeros((1, CELLS), F32)
    for j in range(6):
        named = table_row(j).astype(jnp.int32)
        adj = adj + (ids == named).astype(F32)
        degree = degree + (named < NULL).astype(F32)
    adj_out[...] = adj.astype(BF16)
    sends = jnp.broadcast_to(misc[:, :128], (128, 128)).T
    sends = jnp.concatenate([sends[0:GHOSTS], sends[0:GHOSTS]], axis=1).astype(jnp.int32)
    sel = (sends == lax.broadcasted_iota(jnp.int32, (GHOSTS, CELLS), 1)).astype(F32)
    sel = sel.astype(BF16)
    sel_out[...] = sel
    count = misc[:, GHOSTS : GHOSTS + 1].astype(jnp.int32)
    alive = (lax.broadcasted_iota(jnp.int32, (1, CELLS), 1) < count).astype(F32)
    rows_out[...] = jnp.concatenate(
        [kappa, 1.0 - degree * kappa, alive, jnp.zeros((5, CELLS), F32)], axis=0
    )
    for l in range(LEV):
        x_out[l * MEM : (l + 1) * MEM, :] = pert[l * MEM : (l + 1) * MEM, :] * grad[l : l + 1]
    rims = exact_dot(sel, kappa * x_out[...], ((1,), (1,)))
    rims_out(rims, (r0, r1, r2, r3))


def stay(x, adj, sel, rows, y_out, b_out):
    kappa = rows[0:1, :]
    y = x * rows[1:2, :] + exact_dot(kappa * x, adj[0:CELLS, :], ((1,), (0,)))
    y_out[...] = y
    if b_out is not None:
        b_out[...] = exact_dot(sel[...], kappa * y, ((1,), (1,)))


def first_stay_kernel(x, adj, sel, rows, y_out, b_out, gsel_out, ksel_out):
    stay(x[...], adj, sel, rows, y_out, b_out)
    gsel_out[...] = lax.dot_general(
        sel[...], adj[CELLS:, :], (((1,), (1,)), ((), ())), preferred_element_type=F32
    ).astype(BF16)
    ksel_out[...] = exact_dot(
        sel[...], jnp.broadcast_to(rows[0:1, :], (128, CELLS)), ((1,), (1,))
    )


def rim_kernel(b, gsel, ksel, i0, i1, i2, i3, r0, r1, r2, r3):
    came = joined((i0, i1, i2, i3))
    rims = b[...] + ksel[:, 0:1] * exact_dot(gsel[...], came, ((1,), (0,)))
    rims_out(rims, (r0, r1, r2, r3))


def arrive(y, adj, i0, i1, i2, i3):
    came = joined((i0, i1, i2, i3))
    return y[...] + exact_dot(came.T, adj[CELLS:, :], ((1,), (0,)))


def stay_kernel(y, adj, sel, rows, i0, i1, i2, i3, y_out, b_out=None):
    stay(arrive(y, adj, i0, i1, i2, i3), adj, sel, rows, y_out, b_out)


def mix_kernel(vloc, out):
    level = lax.broadcasted_iota(jnp.int32, (FIELDS, 128), 0) // MEM
    spread = (level == lax.broadcasted_iota(jnp.int32, (FIELDS, 128), 1)).astype(BF16)
    wide = exact_dot(spread[:, 0:LEV], vloc[...].T, ((1,), (0,)))
    full = exact_dot(wide, spread[:, 0:LEV], ((1,), (1,)))
    row = lax.broadcasted_iota(jnp.int32, (FIELDS, FIELDS), 0) % MEM
    column = lax.broadcasted_iota(jnp.int32, (FIELDS, FIELDS), 1) % MEM
    out[...] = jnp.where(row == column, full, 0.0)


def last_kernel(y, adj, rows, mix, i0, i1, i2, i3, out):
    x = arrive(y, adj, i0, i1, i2, i3) * rows[2:3, :]
    out[...] = jnp.dot(
        mix[...], x, precision=lax.Precision.HIGHEST, preferred_element_type=F32
    )


VM = pl.BlockSpec(memory_space=pltpu.VMEM)
SM = pl.BlockSpec(memory_space=pltpu.SMEM)


def call(kernel, shapes, args, scalars=0, flops=10**8, scratch=()):
    specs = [SM] * scalars + [VM] * (len(args) - scalars)
    return pl.pallas_call(
        kernel,
        out_shape=[jax.ShapeDtypeStruct(s, t) for s, t in shapes],
        in_specs=specs,
        out_specs=[VM] * len(shapes),
        scratch_shapes=list(scratch),
        cost_estimate=pl.CostEstimate(flops=flops, bytes_accessed=10**6, transcendentals=0),
        compiler_params=pltpu.CompilerParams(vmem_limit_bytes=32 * 1024 * 1024),
    )(*args)


def exchange(rims):
    return [lax.ppermute(rims[d], AXES, ROUTES[d]) for d in range(4)]


def local(perturbations, gradient, kappa, vloc, neighbors, send_lists, counts):
    fields = perturbations.transpose(1, 0, 2).reshape(FIELDS, CELLS)
    pert = lax.ppermute(fields, AXES, SWAP)
    member = lax.axis_index("member")
    (slots,) = call(
        pack_kernel,
        [((16, SLOT, 128), F32)],
        (
            member.reshape(1),
            counts,
            gradient.reshape(LEV, 32).T,
            kappa.reshape(1, CELLS),
            neighbors,
            send_lists,
        ),
        scalars=2,
        scratch=[pltpu.VMEM((8, CELLS), F32)],
    )
    slots = lax.all_to_all(slots, ("yh", "member"), 0, 0)
    rim_shapes = [((RIM, FIELDS), F32)] * 4
    state = ((FIELDS, CELLS), F32)
    border = ((GHOSTS, FIELDS), F32)
    *rims, x, adj, sel, rows = call(
        first_kernel,
        rim_shapes
        + [state, ((NULL, CELLS), BF16), ((GHOSTS, CELLS), BF16), ((8, CELLS), F32)],
        ((member % 2).reshape(1), slots, pert),
        scalars=1,
    )
    came = exchange(rims)
    y, b, gsel, ksel = call(
        first_stay_kernel,
        [state, border, ((GHOSTS, GHOSTS), BF16), ((GHOSTS, 128), F32)],
        (x, adj, sel, rows),
    )
    for step in range(1, STEPS):
        rims = call(rim_kernel, rim_shapes, (b, gsel, ksel, *came))
        shapes = [state, border] if step < STEPS - 1 else [state]
        y, *b = call(stay_kernel, shapes, (y, adj, sel, rows, *came))
        b = b[0] if b else None
        came = exchange(rims)
    (mix,) = call(mix_kernel, [((FIELDS, FIELDS), F32)], (vloc,))
    (out,) = call(last_kernel, [state], (y, adj, rows, mix, *came))
    out = lax.ppermute(out, AXES, SWAP)
    return out.reshape(LEV, MEM, CELLS).transpose(1, 0, 2)


def solution(mesh):
    near = Mesh(mesh.devices.reshape(8, 4, 2, 8), AXES)
    patch = ("x", "yh", "z")
    return jax.shard_map(
        local,
        mesh=near,
        in_specs=(
            P("member", None, patch),
            P(None, patch, "member"),
            P(patch),
            P(),
            P(None, patch),
            P(None, patch),
            P(patch),
        ),
        out_specs=P("member", None, patch),
        check_vma=False,
    )
```

```python
import itertools

import jax
import jax.numpy as jnp
from jax import lax
from jax.experimental import pallas as pl
from jax.experimental.pallas import tpu as pltpu
from jax.sharding import Mesh
from jax.sharding import PartitionSpec as P

STEPS = 4
AXES = ("member", "x", "yh", "z")
LEV = 55
MEM = 8
FIELDS = LEV * MEM
CELLS = 256
RIM = 16
GHOSTS = 4 * RIM
NULL = CELLS + GHOSTS
F32 = jnp.float32
BF16 = jnp.bfloat16


def flat(x, yh, l, z, core):
    return (l * 2 + core) * 64 + (x % 4) * 16 + yh * 8 + z % 8


def pairs(move):
    every = itertools.product(range(4), range(2), range(4), range(8), range(2))
    return sorted((flat(*c), flat(*move(*c))) for c in every)


def next_column(x, yh, l, z, core):
    if z < 7:
        return x, yh, l, z + 1, core
    return x + core, yh, l, 0, 1 - core


def near(x, yh, l, z, core):
    y = (l + 2 + 4 * core) % 8
    return x, y // 4, y % 4, z, yh


GO = pairs(near)
BACK = sorted((b, a) for a, b in GO)
EAST = pairs(next_column)
WEST = sorted((b, a) for a, b in EAST)
SOUTH = pairs(lambda x, yh, l, z, core: (x + core, yh, l, z, 1 - core))
NORTH = sorted((b, a) for a, b in SOUTH)
ROUTES = (EAST, SOUTH, WEST, NORTH)
ORDER = (0, 2, 1, 3)
HOME = dict(BACK)


def homeward(route):
    return [(a, HOME[b]) for a, b in route]


def split(value, count):
    parts = []
    for _ in range(count):
        parts.append(value.astype(BF16))
        value = value - parts[-1].astype(F32)
    return parts


def exact_dot(left, right, dims, count=2):
    split_left = left.dtype == F32
    total = None
    for part in reversed(split(left if split_left else right, count)):
        a, b = (part, right) if split_left else (left, part)
        term = lax.dot_general(a, b, (dims, ((), ())), preferred_element_type=F32)
        total = term if total is None else total + term
    return total


def chosen(sends):
    column = jnp.broadcast_to(sends, (128, 128)).T[0:GHOSTS].astype(jnp.int32)
    slots = lax.broadcasted_iota(jnp.int32, (GHOSTS, CELLS), 1)
    return (jnp.concatenate([column, column], axis=1) == slots).astype(F32).astype(BF16)


def named_cells(table, adj, rows, kappa):
    ids = lax.broadcasted_iota(jnp.int32, (NULL, CELLS), 0)
    total = jnp.zeros((NULL, CELLS), F32)
    degree = jnp.zeros((1, CELLS), F32)
    for j in range(6):
        named = table[j : j + 1, :].astype(jnp.int32)
        total = total + (ids == named).astype(F32)
        degree = degree + (named < NULL).astype(F32)
    adj[...] = total.astype(BF16)
    rows[...] = jnp.concatenate(
        [kappa, 1.0 - degree * kappa, jnp.zeros((6, CELLS), F32)], axis=0
    )


def pack_kernel(member, grad_in, kappa_in, named_in, sends_in, slots, table, *scratch):
    *held, done = scratch
    copies = [
        pltpu.make_async_copy(here, there, done.at[i])
        for i, (here, there) in enumerate(zip((grad_in, kappa_in, named_in, sends_in), held))
    ]
    for copy in copies:
        copy.start()
    for copy in copies:
        copy.wait()
    grad, kappa, named, sends = held
    table[0:6, :] = named[...].astype(F32)
    table[6:7, :] = kappa[...]
    row = [sends[d : d + 1, :].astype(F32) for d in range(4)]
    row.append(jnp.zeros((1, CELLS - GHOSTS), F32))
    table[7:8, :] = jnp.concatenate(row, axis=1)
    row = table[pl.ds(member[0], 1), :]
    row = jnp.concatenate([row[:, i * 16 : (i + 1) * 16] for i in range(16)], axis=0)
    end = jnp.zeros((RIM, 1), F32)
    slots[0] = jnp.concatenate(
        [grad[0:RIM, :], row[:, 0:8], end, grad[RIM:, :], row[:, 8:16], end], axis=1
    )
    for s in range(1, 16):
        slots[s] = slots[0]


def gathered(core, slots):
    cells = []
    for m in range(MEM):
        two = slots[core[0] * MEM + m]
        cells += [two, pltpu.roll(two, 64, 1)]
    return jnp.concatenate(cells, axis=0)


def table_rows(cells, count):
    size = count * 32
    r = lax.broadcasted_iota(jnp.int32, (size, CELLS), 0)
    c = lax.broadcasted_iota(jnp.int32, (size, CELLS), 1)
    wide = jnp.concatenate([cells[:, LEV : LEV + 8]] * 32, axis=1)
    wide = jnp.where((c // 16 == r % 16) & (c // 8 % 2 == r // 16 % 2), wide, 0.0)
    row = lax.broadcasted_iota(jnp.int32, (16, size), 0)
    cell = lax.broadcasted_iota(jnp.int32, (16, size), 1)
    pick = (row == cell // 32).astype(F32).astype(BF16)
    return exact_dot(pick, wide, ((1,), (0,)), 3)[0:8]


def rims_out(rims, outs):
    for d, out in zip(ORDER, outs):
        out[...] = rims[d * RIM : (d + 1) * RIM]


def joined(arrived):
    return jnp.concatenate([arrived[d][...] for d in ORDER], axis=0)


def first_kernel(core, slots, fields, r0, r1, r2, r3, x, cells_out, table_out):
    cells = gathered(core, slots)
    cells_out[...] = cells
    grad = cells.T
    table = table_rows(cells[192:], 2)
    table_out[...] = table
    for l in range(LEV):
        x[l * MEM : (l + 1) * MEM, :] = fields[l * MEM : (l + 1) * MEM, :] * grad[l : l + 1]
    sel = chosen(table[1:2, :128])
    rims_out(exact_dot(sel, table[0:1, :] * x[...], ((1,), (1,))), (r0, r1, r2, r3))


def stay(x, adj, rows):
    kappa = rows[0:1, :]
    return x * rows[1:2, :] + exact_dot(kappa * x, adj[0:CELLS, :], ((1,), (0,)))


def stay_out(x, adj, sel, rows, y_out, b_out):
    y = stay(x, adj, rows)
    y_out[...] = y
    b_out[...] = exact_dot(sel[...], rows[0:1, :] * y, ((1,), (1,)))


def first_stay_kernel(x, cells, table, y_out, b_out, adj, sel, rows, gsel, ksel):
    named_cells(table_rows(cells[0:192, :], 6), adj, rows, table[0:1, :])
    sel[...] = chosen(table[1:2, :128])
    stay_out(x[...], adj, sel, rows, y_out, b_out)
    gsel[...] = lax.dot_general(
        sel[...], adj[CELLS:, :], (((1,), (1,)), ((), ())), preferred_element_type=F32
    ).astype(BF16)
    kappa = jnp.broadcast_to(table[0:1, :], (128, CELLS))
    ksel[...] = exact_dot(sel[...], kappa, ((1,), (1,)), 3)


def last_rim_kernel(b, gsel, ksel, i3, i0, i1, i2, *outs):
    rim_kernel(b, gsel, ksel, i0, i1, i2, i3, *outs)


def rim_kernel(b, gsel, ksel, i0, i1, i2, i3, r0, r1, r2, r3, came_out):
    came = joined((i0, i1, i2, i3))
    came_out[...] = came
    rims = b[...] + ksel[:, 0:1] * exact_dot(gsel[...], came, ((1,), (0,)), 3)
    rims_out(rims, (r0, r1, r2, r3))


def arrive(y, ghosts, came):
    return y[...] + exact_dot(came.T, ghosts, ((1,), (0,)))


def stay_kernel(y, adj, sel, rows, came, y_out, b_out):
    x = arrive(y, adj[CELLS:, :], came[...])
    stay_out(x, adj, sel, rows, y_out, b_out)


def dot_split(left, right):
    total = jnp.dot(left[1], right[0], preferred_element_type=F32)
    total = total + jnp.dot(left[0], right[1], preferred_element_type=F32)
    return total + jnp.dot(left[0], right[0], preferred_element_type=F32)


def last_stay_kernel(y, adj, rows, mix_high, mix_low, came, out):
    x = arrive(y, adj[CELLS:, :], came[...])
    out[...] = dot_split((mix_high[...], mix_low[...]), split(stay(x, adj, rows), 2))


def mixed_sides(first, second, ghosts, back_high, back_low):
    came = jnp.concatenate([first[...], second[...]], axis=0)
    rims = dot_split(split(came, 2), (back_high[...], back_low[...]))
    return exact_dot(rims.T, ghosts, ((1,), (0,)))


def near_sides_kernel(y, adj, back_high, back_low, south, north, out):
    ghosts = adj[CELLS + 2 * RIM :, :]
    out[...] = y[...] + mixed_sides(south, north, ghosts, back_high, back_low)


def home_sides_kernel(ghosts, back_high, back_low, east, west, out):
    out[...] = mixed_sides(east, west, ghosts[...], back_high, back_low)


def home_kernel(vloc, named, mix_high, mix_low, back_high, back_low, ghosts):
    level = lax.broadcasted_iota(jnp.int32, (FIELDS, 128), 0) // MEM
    spread = level == lax.broadcasted_iota(jnp.int32, (FIELDS, 128), 1)
    spread = spread.astype(F32).astype(BF16)[:, 0:LEV]
    row = lax.broadcasted_iota(jnp.int32, (FIELDS, FIELDS), 0) % MEM
    column = lax.broadcasted_iota(jnp.int32, (FIELDS, FIELDS), 1) % MEM
    for square, outs in ((vloc[...].T, (mix_high, mix_low)), (vloc[...], (back_high, back_low))):
        wide = exact_dot(spread, square, ((1,), (0,)), 3)
        full = exact_dot(wide, spread, ((1,), (1,)), 3)
        for out, part in zip(outs, split(jnp.where(row == column, full, 0.0), 2)):
            out[...] = part
    ids = lax.broadcasted_iota(jnp.int32, (2 * RIM, CELLS), 0) + CELLS
    total = jnp.zeros((2 * RIM, CELLS), F32)
    for j in range(6):
        total = total + (ids == named[j : j + 1, :]).astype(F32)
    ghosts[...] = total.astype(BF16)


def last_kernel(count, y, sides, out):
    alive = lax.broadcasted_iota(jnp.int32, (1, CELLS), 1) < count[0]
    out[...] = jnp.where(alive, y[...] + sides[...], 0.0)


VM = pl.BlockSpec(memory_space=pltpu.VMEM)
SM = pl.BlockSpec(memory_space=pltpu.SMEM)


def call(kernel, shapes, args, scalars=0, flops=10**8, scratch=(), rest=VM):
    specs = [SM] * scalars + [rest] * (len(args) - scalars)
    return pl.pallas_call(
        kernel,
        out_shape=[jax.ShapeDtypeStruct(s, t) for s, t in shapes],
        in_specs=specs,
        out_specs=[VM] * len(shapes),
        scratch_shapes=list(scratch),
        cost_estimate=pl.CostEstimate(flops=flops, bytes_accessed=10**6, transcendentals=0),
        compiler_params=pltpu.CompilerParams(vmem_limit_bytes=32 * 1024 * 1024),
    )(*args)


def exchange(rims):
    return [lax.ppermute(rim, AXES, route) for rim, route in zip(rims, ROUTES)]


def local(perturbations, gradient, kappa, vloc, neighbors, send_lists, counts):
    fields = perturbations.transpose(1, 0, 2).reshape(FIELDS, CELLS)
    state = ((FIELDS, CELLS), F32)
    border = ((GHOSTS, FIELDS), F32)
    rim_shapes = [((RIM, FIELDS), F32)] * 4
    member = lax.axis_index("member")
    (slots,) = call(
        pack_kernel,
        [((16, RIM, 128), F32)],
        (
            member.reshape(1),
            gradient.reshape(LEV, 32).T,
            kappa.reshape(1, CELLS),
            neighbors,
            send_lists,
        ),
        scalars=1,
        scratch=[
            pltpu.VMEM((8, CELLS), F32),
            pltpu.VMEM((32, LEV), F32),
            pltpu.VMEM((1, CELLS), F32),
            pltpu.VMEM((6, CELLS), jnp.int32),
            pltpu.VMEM((4, RIM), jnp.int32),
            pltpu.SemaphoreType.DMA((4,)),
        ],
        rest=pl.BlockSpec(memory_space=pltpu.HBM),
    )
    slots, fields = lax.optimization_barrier((slots, fields))
    fields = lax.ppermute(fields, AXES, GO)
    slots = lax.all_to_all(slots, ("yh", "member"), 0, 0)
    *rims, x, cells, table = call(
        first_kernel,
        rim_shapes + [state, ((CELLS, 128), F32), ((8, CELLS), F32)],
        ((member % 2).reshape(1), slots, fields),
        scalars=1,
    )
    came = exchange(rims)
    y, b, adj, sel, rows, gsel, ksel = call(
        first_stay_kernel,
        [
            state,
            border,
            ((NULL, CELLS), BF16),
            ((GHOSTS, CELLS), BF16),
            ((8, CELLS), F32),
            ((GHOSTS, GHOSTS), BF16),
            ((GHOSTS, 128), F32),
        ],
        (x, cells, table),
    )
    square = ((FIELDS, FIELDS), BF16)
    mix_high, mix_low, back_high, back_low, ghosts = call(
        home_kernel, [square] * 4 + [((2 * RIM, CELLS), BF16)], (vloc, neighbors)
    )
    for step in range(1, STEPS - 1):
        *rims, came = call(rim_kernel, rim_shapes + [border], (b, gsel, ksel, *came))
        y, b = call(stay_kernel, [state, border], (y, adj, sel, rows, came))
        came = exchange(rims)
    east, south, west, north, came = call(
        last_rim_kernel, rim_shapes + [border], (b, gsel, ksel, came[3], *came[:3])
    )
    (y,) = call(last_stay_kernel, [state], (y, adj, rows, mix_high, mix_low, came))
    south = lax.ppermute(south, AXES, SOUTH)
    north = lax.ppermute(north, AXES, NORTH)
    (y,) = call(near_sides_kernel, [state], (y, adj, back_high, back_low, south, north))
    y, east, west = lax.optimization_barrier((y, east, west))
    y = lax.ppermute(y, AXES, BACK)
    east = lax.ppermute(east, AXES, homeward(EAST))
    west = lax.ppermute(west, AXES, homeward(WEST))
    (sides,) = call(home_sides_kernel, [state], (ghosts, back_high, back_low, east, west))
    (out,) = call(last_kernel, [state], (counts, y, sides), scalars=1)
    return out.reshape(LEV, MEM, CELLS).transpose(1, 0, 2)


def solution(mesh):
    parts = Mesh(mesh.devices.reshape(8, 4, 2, 8), AXES)
    patch = ("x", "yh", "z")
    return jax.shard_map(
        local,
        mesh=parts,
        in_specs=(
            P("member", None, patch),
            P(None, patch, "member"),
            P(patch),
            P(),
            P(None, patch),
            P(None, patch),
            P(patch),
        ),
        out_specs=P("member", None, patch),
        check_vma=False,
    )
```

```python
import itertools

import jax
import jax.numpy as jnp
from jax import lax
from jax.experimental import pallas as pl
from jax.experimental.pallas import tpu as pltpu
from jax.sharding import Mesh
from jax.sharding import PartitionSpec as P

STEPS = 4
AXES = ("member", "x", "yh", "z")
LEV = 55
MEM = 8
FIELDS = LEV * MEM
CELLS = 256
RIM = 16
GHOSTS = 4 * RIM
NULL = CELLS + GHOSTS
F32 = jnp.float32
BF16 = jnp.bfloat16


def flat(x, yh, l, z, core):
    return (l * 2 + core) * 64 + (x % 4) * 16 + yh * 8 + z % 8


def pairs(move):
    every = itertools.product(range(4), range(2), range(4), range(8), range(2))
    return sorted((flat(*c), flat(*move(*c))) for c in every)


def next_column(x, yh, l, z, core):
    if z < 7:
        return x, yh, l, z + 1, core
    return x + core, yh, l, 0, 1 - core


def near(x, yh, l, z, core):
    y = (l + 2 + 4 * core) % 8
    return x, y // 4, y % 4, z, yh


GO = pairs(near)
BACK = sorted((b, a) for a, b in GO)
EAST = pairs(next_column)
WEST = sorted((b, a) for a, b in EAST)
SOUTH = pairs(lambda x, yh, l, z, core: (x + core, yh, l, z, 1 - core))
NORTH = sorted((b, a) for a, b in SOUTH)
ROUTES = (EAST, SOUTH, WEST, NORTH)
ORDER = (0, 2, 1, 3)
HOME = dict(BACK)


def homeward(route):
    return [(a, HOME[b]) for a, b in route]


def split(value, count):
    parts = []
    for _ in range(count):
        parts.append(value.astype(BF16))
        value = value - parts[-1].astype(F32)
    return parts


def exact_dot(left, right, dims, count=2):
    split_left = left.dtype == F32
    total = None
    for part in reversed(split(left if split_left else right, count)):
        a, b = (part, right) if split_left else (left, part)
        term = lax.dot_general(a, b, (dims, ((), ())), preferred_element_type=F32)
        total = term if total is None else total + term
    return total


def chosen(sends):
    column = jnp.broadcast_to(sends, (128, 128)).T[0:GHOSTS].astype(jnp.int32)
    slots = lax.broadcasted_iota(jnp.int32, (GHOSTS, CELLS), 1)
    return (jnp.concatenate([column, column], axis=1) == slots).astype(F32).astype(BF16)


def named_cells(table, adj, rows, kappa):
    ids = lax.broadcasted_iota(jnp.int32, (NULL, CELLS), 0)
    total = jnp.zeros((NULL, CELLS), F32)
    degree = jnp.zeros((1, CELLS), F32)
    for j in range(6):
        named = table[j : j + 1, :].astype(jnp.int32)
        total = total + (ids == named).astype(F32)
        degree = degree + (named < NULL).astype(F32)
    adj[...] = total.astype(BF16)
    rows[...] = jnp.concatenate(
        [kappa, 1.0 - degree * kappa, jnp.zeros((6, CELLS), F32)], axis=0
    )


def pack_kernel(grad_in, fields_in, kappa_in, named_in, sends_in, slots, out, *scratch):
    *held, done = scratch
    given = (grad_in, fields_in, kappa_in, named_in, sends_in)
    copies = [
        pltpu.make_async_copy(here, there, done.at[i])
        for i, (here, there) in enumerate(zip(given, held))
    ]
    for copy in copies:
        copy.start()
    for copy in copies:
        copy.wait()
    grad, fields, kappa, named, sends = held
    piece = jnp.concatenate([grad[...], jnp.zeros((32, 64 - LEV), F32)], axis=1)
    slots[0] = jnp.concatenate([piece[0:RIM], piece[RIM:]], axis=1)
    for s in range(1, 16):
        slots[s] = slots[0]
    row = [sends[d : d + 1, :].astype(F32) for d in range(4)]
    row.append(jnp.zeros((1, CELLS - GHOSTS), F32))
    row = jnp.concatenate(row, axis=1)
    out[0:GHOSTS, :] = exact_dot(chosen(row[:, :128]), fields[...], ((1,), (1,)), 3)
    out[GHOSTS:, 0:CELLS] = jnp.concatenate([named[...].astype(F32), kappa[...], row], axis=0)
    out[GHOSTS:, CELLS:] = jnp.zeros((8, FIELDS - CELLS), F32)


def near_kernel(load, adj, sel, rows, gsel, ksel):
    table = load[GHOSTS:, 0:CELLS]
    named_cells(table, adj, rows, table[6:7, :])
    sel[...] = chosen(table[7:8, :128])
    gsel[...] = lax.dot_general(
        sel[...], adj[CELLS:, :], (((1,), (1,)), ((), ())), preferred_element_type=F32
    ).astype(BF16)
    kappa = jnp.broadcast_to(table[6:7, :], (128, CELLS))
    ksel[...] = exact_dot(sel[...], kappa, ((1,), (1,)), 3)


def gathered(core, slots):
    cells = []
    for m in range(MEM):
        two = slots[core[0] * MEM + m]
        cells += [two, pltpu.roll(two, 64, 1)]
    return jnp.concatenate(cells, axis=0)


def rims_out(rims, outs):
    for d, out in zip(ORDER, outs):
        out[...] = rims[d * RIM : (d + 1) * RIM]


def joined(arrived):
    return jnp.concatenate([arrived[d][...] for d in ORDER], axis=0)


def spread():
    level = lax.broadcasted_iota(jnp.int32, (FIELDS, 128), 0) // MEM
    return (level == lax.broadcasted_iota(jnp.int32, (FIELDS, 128), 1)).astype(F32).astype(BF16)


def first_kernel(core, slots, load, sel, ksel, r0, r1, r2, r3):
    grad = exact_dot(sel[...], gathered(core, slots), ((1,), (0,)), 3)
    lane = lax.broadcasted_iota(jnp.int32, (GHOSTS, 128), 1)
    grad = jnp.where(lane < LEV, grad, 0.0) * ksel[...]
    grad = exact_dot(grad, spread(), ((1,), (1,)), 3)
    rims_out(load[0:GHOSTS, :] * grad, (r0, r1, r2, r3))


def stay(x, adj, rows):
    kappa = rows[0:1, :]
    return x * rows[1:2, :] + exact_dot(kappa * x, adj[0:CELLS, :], ((1,), (0,)))


def stay_out(x, adj, sel, rows, y_out, b_out):
    y = stay(x, adj, rows)
    y_out[...] = y
    b_out[...] = exact_dot(sel[...], rows[0:1, :] * y, ((1,), (1,)))


def first_stay_kernel(core, slots, fields, adj, sel, rows, y_out, b_out, x):
    grad = gathered(core, slots).T
    for l in range(LEV):
        x[l * MEM : (l + 1) * MEM, :] = fields[l * MEM : (l + 1) * MEM, :] * grad[l : l + 1]
    stay_out(x[...], adj, sel, rows, y_out, b_out)


def rim_kernel(b, gsel, ksel, i0, i1, i2, i3, r0, r1, r2, r3, came_out):
    came = joined((i0, i1, i2, i3))
    came_out[...] = came
    rims = b[...] + ksel[:, 0:1] * exact_dot(gsel[...], came, ((1,), (0,)), 3)
    rims_out(rims, (r0, r1, r2, r3))


def arrive(y, ghosts, came):
    return y[...] + exact_dot(came.T, ghosts, ((1,), (0,)))


def stay_kernel(y, adj, sel, rows, came, y_out, b_out):
    x = arrive(y, adj[CELLS:, :], came[...])
    stay_out(x, adj, sel, rows, y_out, b_out)


def dot_split(left, right):
    total = jnp.dot(left[1], right[0], preferred_element_type=F32)
    total = total + jnp.dot(left[0], right[1], preferred_element_type=F32)
    return total + jnp.dot(left[0], right[0], preferred_element_type=F32)


def last_stay_kernel(y, adj, rows, mix_high, mix_low, came, out):
    x = arrive(y, adj[CELLS:, :], came[...])
    out[...] = dot_split((mix_high[...], mix_low[...]), split(stay(x, adj, rows), 2))


def mixed_rims(first, second, back_high, back_low):
    came = jnp.concatenate([first[...], second[...]], axis=0)
    return dot_split(split(came, 2), (back_high[...], back_low[...]))


def near_sides_kernel(y, adj, back_high, back_low, south, north, out):
    rims = mixed_rims(south, north, back_high, back_low)
    out[...] = arrive(y, adj[CELLS + 2 * RIM :, :], rims)


def mix_sides_kernel(back_high, back_low, east, west, east_out, west_out):
    rims = mixed_rims(east, west, back_high, back_low)
    east_out[...] = rims[0:RIM]
    west_out[...] = rims[RIM:]


def home_kernel(vloc, named, mix_high, mix_low, back_high, back_low, ghosts):
    level = lax.broadcasted_iota(jnp.int32, (FIELDS, 128), 0) // MEM
    spread = level == lax.broadcasted_iota(jnp.int32, (FIELDS, 128), 1)
    spread = spread.astype(F32).astype(BF16)[:, 0:LEV]
    row = lax.broadcasted_iota(jnp.int32, (FIELDS, FIELDS), 0) % MEM
    column = lax.broadcasted_iota(jnp.int32, (FIELDS, FIELDS), 1) % MEM
    for square, outs in ((vloc[...].T, (mix_high, mix_low)), (vloc[...], (back_high, back_low))):
        wide = exact_dot(spread, square, ((1,), (0,)), 3)
        full = exact_dot(wide, spread, ((1,), (1,)), 3)
        for out, part in zip(outs, split(jnp.where(row == column, full, 0.0), 2)):
            out[...] = part
    ids = lax.broadcasted_iota(jnp.int32, (2 * RIM, CELLS), 0) + CELLS
    total = jnp.zeros((2 * RIM, CELLS), F32)
    for j in range(6):
        total = total + (ids == named[j : j + 1, :]).astype(F32)
    ghosts[...] = total.astype(BF16)


def last_kernel(count, y, ghosts, east, west, out):
    alive = lax.broadcasted_iota(jnp.int32, (1, CELLS), 1) < count[0]
    rims = jnp.concatenate([east[...], west[...]], axis=0)
    out[...] = jnp.where(alive, arrive(y, ghosts[...], rims), 0.0)


VM = pl.BlockSpec(memory_space=pltpu.VMEM)
SM = pl.BlockSpec(memory_space=pltpu.SMEM)


def call(kernel, shapes, args, scalars=0, flops=10**8, scratch=(), rest=VM, vmem=32):
    specs = [SM] * scalars + [rest] * (len(args) - scalars)
    return pl.pallas_call(
        kernel,
        out_shape=[jax.ShapeDtypeStruct(s, t) for s, t in shapes],
        in_specs=specs,
        out_specs=[VM] * len(shapes),
        scratch_shapes=list(scratch),
        cost_estimate=pl.CostEstimate(flops=flops, bytes_accessed=10**6, transcendentals=0),
        compiler_params=pltpu.CompilerParams(vmem_limit_bytes=vmem * 1024 * 1024),
    )(*args)


def exchange(rims):
    return [lax.ppermute(rim, AXES, route) for rim, route in zip(rims, ROUTES)]


def local(perturbations, gradient, kappa, vloc, neighbors, send_lists, counts):
    fields = perturbations.transpose(1, 0, 2).reshape(FIELDS, CELLS)
    state = ((FIELDS, CELLS), F32)
    border = ((GHOSTS, FIELDS), F32)
    rim_shapes = [((RIM, FIELDS), F32)] * 4
    core = (lax.axis_index("member") % 2).reshape(1)
    slots, load = call(
        pack_kernel,
        [((16, RIM, 128), F32), ((GHOSTS + 8, FIELDS), F32)],
        (
            gradient.reshape(LEV, 32).T,
            fields,
            kappa.reshape(1, CELLS),
            neighbors,
            send_lists,
        ),
        scratch=[
            pltpu.VMEM((32, LEV), F32),
            pltpu.VMEM((FIELDS, CELLS), F32),
            pltpu.VMEM((1, CELLS), F32),
            pltpu.VMEM((6, CELLS), jnp.int32),
            pltpu.VMEM((4, RIM), jnp.int32),
            pltpu.SemaphoreType.DMA((5,)),
        ],
        rest=pl.BlockSpec(memory_space=pltpu.HBM),
        vmem=60,
    )
    load = lax.ppermute(load, AXES, GO)
    slots = lax.all_to_all(slots, ("yh", "member"), 0, 0)
    square = ((FIELDS, FIELDS), BF16)
    mix_high, mix_low, back_high, back_low, ghosts = call(
        home_kernel, [square] * 4 + [((2 * RIM, CELLS), BF16)], (vloc, neighbors)
    )
    adj, sel, rows, gsel, ksel = call(
        near_kernel,
        [
            ((NULL, CELLS), BF16),
            ((GHOSTS, CELLS), BF16),
            ((8, CELLS), F32),
            ((GHOSTS, GHOSTS), BF16),
            ((GHOSTS, 128), F32),
        ],
        (load,),
        flops=10**10,
    )
    gsel, fields = lax.optimization_barrier((gsel, fields))
    fields = lax.ppermute(fields, AXES, GO)
    rims = call(
        first_kernel, rim_shapes, (core, slots, load, sel, ksel), scalars=1, flops=2*10**10
    )
    came = exchange(rims)
    y, b = call(
        first_stay_kernel,
        [state, border],
        (core, slots, fields, adj, sel, rows),
        scalars=1,
        scratch=[pltpu.VMEM((FIELDS, CELLS), F32)],
    )
    for step in range(1, STEPS - 1):
        *rims, came = call(rim_kernel, rim_shapes + [border], (b, gsel, ksel, *came))
        y, b = call(stay_kernel, [state, border], (y, adj, sel, rows, came))
        came = exchange(rims)
        if step == 1:
            came[0], ghosts = lax.optimization_barrier((came[0], ghosts))
    east, south, west, north, came = call(
        rim_kernel, rim_shapes + [border], (b, gsel, ksel, *came)
    )
    (y,) = call(last_stay_kernel, [state], (y, adj, rows, mix_high, mix_low, came))
    south = lax.ppermute(south, AXES, SOUTH)
    north = lax.ppermute(north, AXES, NORTH)
    east, west = call(mix_sides_kernel, rim_shapes[:2], (back_high, back_low, east, west))
    (y,) = call(near_sides_kernel, [state], (y, adj, back_high, back_low, south, north))
    y, east, west = lax.optimization_barrier((y, east, west))
    y = lax.ppermute(y, AXES, BACK)
    east = lax.ppermute(east, AXES, homeward(EAST))
    west = lax.ppermute(west, AXES, homeward(WEST))
    (out,) = call(last_kernel, [state], (counts, y, ghosts, east, west), scalars=1)
    return out.reshape(LEV, MEM, CELLS).transpose(1, 0, 2)


def solution(mesh):
    parts = Mesh(mesh.devices.reshape(8, 4, 2, 8), AXES)
    patch = ("x", "yh", "z")
    return jax.shard_map(
        local,
        mesh=parts,
        in_specs=(
            P("member", None, patch),
            P(None, patch, "member"),
            P(patch),
            P(),
            P(None, patch),
            P(None, patch),
            P(patch),
        ),
        out_specs=P("member", None, patch),
        check_vma=False,
    )
```

```python
import itertools

import jax
import jax.numpy as jnp
from jax import lax
from jax.experimental import pallas as pl
from jax.experimental.pallas import tpu as pltpu
from jax.sharding import Mesh
from jax.sharding import PartitionSpec as P

STEPS = 4
AXES = ("member", "x", "yh", "z")
LEV = 55
MEM = 8
FIELDS = LEV * MEM
CELLS = 256
RIM = 16
GHOSTS = 4 * RIM
NULL = CELLS + GHOSTS
F32 = jnp.float32
BF16 = jnp.bfloat16


def flat(x, yh, l, z, core):
    return (l * 2 + core) * 64 + (x % 4) * 16 + yh * 8 + z % 8


def pairs(move):
    every = itertools.product(range(4), range(2), range(4), range(8), range(2))
    return sorted((flat(*c), flat(*move(*c))) for c in every)


def next_column(x, yh, l, z, core):
    if z < 7:
        return x, yh, l, z + 1, core
    return x + core, yh, l, 0, 1 - core


def near(x, yh, l, z, core):
    y = (l + 2 + 4 * core) % 8
    return x, y // 4, y % 4, z, yh


GO = pairs(near)
BACK = sorted((b, a) for a, b in GO)
EAST = pairs(next_column)
WEST = sorted((b, a) for a, b in EAST)
SOUTH = pairs(lambda x, yh, l, z, core: (x + core, yh, l, z, 1 - core))
NORTH = sorted((b, a) for a, b in SOUTH)
ROUTES = (EAST, SOUTH, WEST, NORTH)
ORDER = (0, 2, 1, 3)
HOME = dict(BACK)


def homeward(route):
    return [(a, HOME[b]) for a, b in route]


def split(value, count):
    parts = []
    for _ in range(count):
        parts.append(value.astype(BF16))
        value = value - parts[-1].astype(F32)
    return parts


def exact_dot(left, right, dims, count=2):
    split_left = left.dtype == F32
    total = None
    for part in reversed(split(left if split_left else right, count)):
        a, b = (part, right) if split_left else (left, part)
        term = lax.dot_general(a, b, (dims, ((), ())), preferred_element_type=F32)
        total = term if total is None else total + term
    return total


def chosen(sends):
    column = jnp.broadcast_to(sends, (128, 128)).T[0:GHOSTS].astype(jnp.int32)
    slots = lax.broadcasted_iota(jnp.int32, (GHOSTS, CELLS), 1)
    return (jnp.concatenate([column, column], axis=1) == slots).astype(F32).astype(BF16)


def named_cells(table, adj, rows, kappa):
    ids = lax.broadcasted_iota(jnp.int32, (NULL, CELLS), 0)
    total = jnp.zeros((NULL, CELLS), F32)
    degree = jnp.zeros((1, CELLS), F32)
    for j in range(6):
        named = table[j : j + 1, :].astype(jnp.int32)
        total = total + (ids == named).astype(F32)
        degree = degree + (named < NULL).astype(F32)
    adj[...] = total.astype(BF16)
    rows[...] = jnp.concatenate(
        [kappa, 1.0 - degree * kappa, jnp.zeros((6, CELLS), F32)], axis=0
    )


def pack_kernel(grad_in, fields_in, kappa_in, named_in, sends_in, slots, out, *scratch):
    *held, done = scratch
    given = (grad_in, fields_in, kappa_in, named_in, sends_in)
    copies = [
        pltpu.make_async_copy(here, there, done.at[i])
        for i, (here, there) in enumerate(zip(given, held))
    ]
    for copy in copies:
        copy.start()
    for copy in copies:
        copy.wait()
    grad, fields, kappa, named, sends = held
    piece = jnp.concatenate([grad[...], jnp.zeros((32, 64 - LEV), F32)], axis=1)
    slots[0] = jnp.concatenate([piece[0:RIM], piece[RIM:]], axis=1)
    for s in range(1, 16):
        slots[s] = slots[0]
    row = [sends[d : d + 1, :].astype(F32) for d in range(4)]
    row.append(jnp.zeros((1, CELLS - GHOSTS), F32))
    row = jnp.concatenate(row, axis=1)
    out[0:GHOSTS, :] = exact_dot(chosen(row[:, :128]), fields[...], ((1,), (1,)), 3)
    out[GHOSTS:, 0:CELLS] = jnp.concatenate([named[...].astype(F32), kappa[...], row], axis=0)
    out[GHOSTS:, CELLS:] = jnp.zeros((8, FIELDS - CELLS), F32)


def near_kernel(load, adj, sel, rows, gsel, ksel):
    table = load[GHOSTS:, 0:CELLS]
    named_cells(table, adj, rows, table[6:7, :])
    sel[...] = chosen(table[7:8, :128])
    gsel[...] = lax.dot_general(
        sel[...], adj[CELLS:, :], (((1,), (1,)), ((), ())), preferred_element_type=F32
    ).astype(BF16)
    kappa = jnp.broadcast_to(table[6:7, :], (128, CELLS))
    ksel[...] = exact_dot(sel[...], kappa, ((1,), (1,)), 3)


def gathered(core, slots):
    cells = []
    for m in range(MEM):
        two = slots[core[0] * MEM + m]
        cells += [two, pltpu.roll(two, 64, 1)]
    return jnp.concatenate(cells, axis=0)


def rims_out(rims, outs):
    for d, out in zip(ORDER, outs):
        out[...] = rims[d * RIM : (d + 1) * RIM]


def joined(arrived):
    return jnp.concatenate([arrived[d][...] for d in ORDER], axis=0)


def spread():
    level = lax.broadcasted_iota(jnp.int32, (FIELDS, 128), 0) // MEM
    return (level == lax.broadcasted_iota(jnp.int32, (FIELDS, 128), 1)).astype(F32).astype(BF16)


def first_kernel(core, slots, load, sel, ksel, r0, r1, r2, r3):
    grad = exact_dot(sel[...], gathered(core, slots), ((1,), (0,)), 3)
    lane = lax.broadcasted_iota(jnp.int32, (GHOSTS, 128), 1)
    grad = jnp.where(lane < LEV, grad, 0.0) * ksel[...]
    grad = exact_dot(grad, spread(), ((1,), (1,)), 3)
    rims_out(load[0:GHOSTS, :] * grad, (r0, r1, r2, r3))


def stay(x, adj, rows):
    kappa = rows[0:1, :]
    return x * rows[1:2, :] + exact_dot(kappa * x, adj[0:CELLS, :], ((1,), (0,)))


def stay_out(x, adj, sel, rows, y_out, b_out):
    y = stay(x, adj, rows)
    y_out[...] = y
    b_out[...] = exact_dot(sel[...], rows[0:1, :] * y, ((1,), (1,)))


def first_stay_kernel(core, slots, fields, adj, sel, rows, y_out, b_out, x):
    grad = gathered(core, slots).T
    for l in range(LEV):
        x[l * MEM : (l + 1) * MEM, :] = fields[l * MEM : (l + 1) * MEM, :] * grad[l : l + 1]
    stay_out(x[...], adj, sel, rows, y_out, b_out)


def rim_kernel(b, gsel, ksel, i0, i1, i2, i3, r0, r1, r2, r3, came_out):
    came = joined((i0, i1, i2, i3))
    came_out[...] = came
    rims = b[...] + ksel[:, 0:1] * exact_dot(gsel[...], came, ((1,), (0,)), 3)
    rims_out(rims, (r0, r1, r2, r3))


def arrive(y, ghosts, came):
    return y[...] + exact_dot(came.T, ghosts, ((1,), (0,)))


def stay_kernel(y, adj, sel, rows, came, y_out, b_out):
    x = arrive(y, adj[CELLS:, :], came[...])
    stay_out(x, adj, sel, rows, y_out, b_out)


def dot_split(left, right):
    total = jnp.dot(left[1], right[0], preferred_element_type=F32)
    total = total + jnp.dot(left[0], right[1], preferred_element_type=F32)
    return total + jnp.dot(left[0], right[0], preferred_element_type=F32)


def last_stay_kernel(y, adj, rows, mix_high, mix_low, came, out):
    x = arrive(y, adj[CELLS:, :], came[...])
    out[...] = dot_split((mix_high[...], mix_low[...]), split(stay(x, adj, rows), 2))


def mixed_rims(first, second, back_high, back_low):
    came = jnp.concatenate([first[...], second[...]], axis=0)
    return dot_split(split(came, 2), (back_high[...], back_low[...]))


def near_sides_kernel(y, adj, back_high, back_low, south, north, out):
    rims = mixed_rims(south, north, back_high, back_low)
    out[...] = arrive(y, adj[CELLS + 2 * RIM :, :], rims)


def mix_sides_kernel(back_high, back_low, east, west, east_out, west_out):
    rims = mixed_rims(east, west, back_high, back_low)
    east_out[...] = rims[0:RIM]
    west_out[...] = rims[RIM:]


def home_kernel(vloc, named, mix_high, mix_low, back_high, back_low, ghosts):
    level = lax.broadcasted_iota(jnp.int32, (FIELDS, 128), 0) // MEM
    spread = level == lax.broadcasted_iota(jnp.int32, (FIELDS, 128), 1)
    spread = spread.astype(F32).astype(BF16)[:, 0:LEV]
    row = lax.broadcasted_iota(jnp.int32, (FIELDS, FIELDS), 0) % MEM
    column = lax.broadcasted_iota(jnp.int32, (FIELDS, FIELDS), 1) % MEM
    for square, outs in ((vloc[...].T, (mix_high, mix_low)), (vloc[...], (back_high, back_low))):
        wide = exact_dot(spread, square, ((1,), (0,)), 3)
        full = exact_dot(wide, spread, ((1,), (1,)), 3)
        for out, part in zip(outs, split(jnp.where(row == column, full, 0.0), 2)):
            out[...] = part
    ids = lax.broadcasted_iota(jnp.int32, (2 * RIM, CELLS), 0) + CELLS
    total = jnp.zeros((2 * RIM, CELLS), F32)
    for j in range(6):
        total = total + (ids == named[j : j + 1, :]).astype(F32)
    ghosts[...] = total.astype(BF16)


def last_kernel(count, y, ghosts, east, west, out):
    alive = lax.broadcasted_iota(jnp.int32, (1, CELLS), 1) < count[0]
    rims = jnp.concatenate([east[...], west[...]], axis=0)
    out[...] = jnp.where(alive, arrive(y, ghosts[...], rims), 0.0)


VM = pl.BlockSpec(memory_space=pltpu.VMEM)
SM = pl.BlockSpec(memory_space=pltpu.SMEM)


def call(kernel, shapes, args, scalars=0, flops=10**8, scratch=(), rest=VM, vmem=32):
    specs = [SM] * scalars + [rest] * (len(args) - scalars)
    return pl.pallas_call(
        kernel,
        out_shape=[jax.ShapeDtypeStruct(s, t) for s, t in shapes],
        in_specs=specs,
        out_specs=[VM] * len(shapes),
        scratch_shapes=list(scratch),
        cost_estimate=pl.CostEstimate(flops=flops, bytes_accessed=10**6, transcendentals=0),
        compiler_params=pltpu.CompilerParams(vmem_limit_bytes=vmem * 1024 * 1024),
    )(*args)


def exchange(rims):
    return [lax.ppermute(rim, AXES, route) for rim, route in zip(rims, ROUTES)]


def local(perturbations, gradient, kappa, vloc, neighbors, send_lists, counts):
    fields = perturbations.transpose(1, 0, 2).reshape(FIELDS, CELLS)
    state = ((FIELDS, CELLS), F32)
    border = ((GHOSTS, FIELDS), F32)
    rim_shapes = [((RIM, FIELDS), F32)] * 4
    core = (lax.axis_index("member") % 2).reshape(1)
    slots, load = call(
        pack_kernel,
        [((16, RIM, 128), F32), ((GHOSTS + 8, FIELDS), F32)],
        (
            gradient.reshape(LEV, 32).T,
            fields,
            kappa.reshape(1, CELLS),
            neighbors,
            send_lists,
        ),
        scratch=[
            pltpu.VMEM((32, LEV), F32),
            pltpu.VMEM((FIELDS, CELLS), F32),
            pltpu.VMEM((1, CELLS), F32),
            pltpu.VMEM((6, CELLS), jnp.int32),
            pltpu.VMEM((4, RIM), jnp.int32),
            pltpu.SemaphoreType.DMA((5,)),
        ],
        rest=pl.BlockSpec(memory_space=pltpu.HBM),
        vmem=60,
    )
    load = lax.ppermute(load, AXES, GO)
    load, fields = lax.optimization_barrier((load, fields))
    fields = lax.ppermute(fields, AXES, GO)
    slots = lax.all_to_all(slots, ("yh", "member"), 0, 0)
    adj, sel, rows, gsel, ksel = call(
        near_kernel,
        [
            ((NULL, CELLS), BF16),
            ((GHOSTS, CELLS), BF16),
            ((8, CELLS), F32),
            ((GHOSTS, GHOSTS), BF16),
            ((GHOSTS, 128), F32),
        ],
        (load,),
        flops=10**10,
    )
    gsel, vloc = lax.optimization_barrier((gsel, vloc))
    square = ((FIELDS, FIELDS), BF16)
    mix_high, mix_low, back_high, back_low, ghosts = call(
        home_kernel, [square] * 4 + [((2 * RIM, CELLS), BF16)], (vloc, neighbors)
    )
    sel, ghosts = lax.optimization_barrier((sel, ghosts))
    rims = call(
        first_kernel, rim_shapes, (core, slots, load, sel, ksel), scalars=1, flops=2*10**10
    )
    came = exchange(rims)
    y, b = call(
        first_stay_kernel,
        [state, border],
        (core, slots, fields, adj, sel, rows),
        scalars=1,
        scratch=[pltpu.VMEM((FIELDS, CELLS), F32)],
    )
    for step in range(1, STEPS - 1):
        *rims, came = call(rim_kernel, rim_shapes + [border], (b, gsel, ksel, *came))
        y, b = call(stay_kernel, [state, border], (y, adj, sel, rows, came))
        came = exchange(rims)
    east, south, west, north, came = call(
        rim_kernel, rim_shapes + [border], (b, gsel, ksel, *came)
    )
    (y,) = call(last_stay_kernel, [state], (y, adj, rows, mix_high, mix_low, came))
    south = lax.ppermute(south, AXES, SOUTH)
    north = lax.ppermute(north, AXES, NORTH)
    east, west = call(mix_sides_kernel, rim_shapes[:2], (back_high, back_low, east, west))
    (y,) = call(near_sides_kernel, [state], (y, adj, back_high, back_low, south, north))
    y, east, west = lax.optimization_barrier((y, east, west))
    y = lax.ppermute(y, AXES, BACK)
    east = lax.ppermute(east, AXES, homeward(EAST))
    west = lax.ppermute(west, AXES, homeward(WEST))
    (out,) = call(last_kernel, [state], (counts, y, ghosts, east, west), scalars=1)
    return out.reshape(LEV, MEM, CELLS).transpose(1, 0, 2)


def solution(mesh):
    parts = Mesh(mesh.devices.reshape(8, 4, 2, 8), AXES)
    patch = ("x", "yh", "z")
    return jax.shard_map(
        local,
        mesh=parts,
        in_specs=(
            P("member", None, patch),
            P(None, patch, "member"),
            P(patch),
            P(),
            P(None, patch),
            P(None, patch),
            P(patch),
        ),
        out_specs=P("member", None, patch),
        check_vma=False,
    )
```

```python
import itertools

import jax
import jax.numpy as jnp
from jax import lax
from jax.experimental import pallas as pl
from jax.experimental.pallas import tpu as pltpu
from jax.sharding import Mesh
from jax.sharding import PartitionSpec as P

STEPS = 4
AXES = ("member", "x", "yh", "z")
LEV = 55
MEM = 8
FIELDS = LEV * MEM
CELLS = 256
RIM = 16
GHOSTS = 4 * RIM
NULL = CELLS + GHOSTS
F32 = jnp.float32
BF16 = jnp.bfloat16


def flat(x, yh, l, z, core):
    return (l * 2 + core) * 64 + (x % 4) * 16 + yh * 8 + z % 8


def pairs(move):
    every = itertools.product(range(4), range(2), range(4), range(8), range(2))
    return sorted((flat(*c), flat(*move(*c))) for c in every)


def next_column(x, yh, l, z, core):
    if z < 7:
        return x, yh, l, z + 1, core
    return x + core, yh, l, 0, 1 - core


def near(x, yh, l, z, core):
    y = (l + 2 + 4 * core) % 8
    return x, y // 4, y % 4, z, yh


GO = pairs(near)
BACK = sorted((b, a) for a, b in GO)
EAST = pairs(next_column)
WEST = sorted((b, a) for a, b in EAST)
SOUTH = pairs(lambda x, yh, l, z, core: (x + core, yh, l, z, 1 - core))
NORTH = sorted((b, a) for a, b in SOUTH)
ROUTES = (EAST, SOUTH, WEST, NORTH)
ORDER = (0, 2, 1, 3)
HOME = dict(BACK)


def homeward(route):
    return [(a, HOME[b]) for a, b in route]


def split(value, count):
    parts = []
    for _ in range(count):
        parts.append(value.astype(BF16))
        value = value - parts[-1].astype(F32)
    return parts


def exact_dot(left, right, dims, count=2):
    split_left = left.dtype == F32
    total = None
    for part in reversed(split(left if split_left else right, count)):
        a, b = (part, right) if split_left else (left, part)
        term = lax.dot_general(a, b, (dims, ((), ())), preferred_element_type=F32)
        total = term if total is None else total + term
    return total


def chosen(sends):
    column = jnp.broadcast_to(sends, (128, 128)).T[0:GHOSTS].astype(jnp.int32)
    slots = lax.broadcasted_iota(jnp.int32, (GHOSTS, CELLS), 1)
    return (jnp.concatenate([column, column], axis=1) == slots).astype(F32).astype(BF16)


def named_cells(table, adj, rows, kappa):
    ids = lax.broadcasted_iota(jnp.int32, (NULL, CELLS), 0)
    total = jnp.zeros((NULL, CELLS), F32)
    degree = jnp.zeros((1, CELLS), F32)
    for j in range(6):
        named = table[j : j + 1, :].astype(jnp.int32)
        total = total + (ids == named).astype(F32)
        degree = degree + (named < NULL).astype(F32)
    adj[...] = total.astype(BF16)
    rows[...] = jnp.concatenate(
        [kappa, 1.0 - degree * kappa, jnp.zeros((6, CELLS), F32)], axis=0
    )


def pack_kernel(grad_in, fields_in, kappa_in, named_in, sends_in, slots, out, *scratch):
    *held, done = scratch
    given = (grad_in, fields_in, kappa_in, named_in, sends_in)
    copies = [
        pltpu.make_async_copy(here, there, done.at[i])
        for i, (here, there) in enumerate(zip(given, held))
    ]
    for copy in copies:
        copy.start()
    grad, fields, kappa, named, sends = held
    copies[0].wait()
    piece = jnp.concatenate([grad[...], jnp.zeros((32, 64 - LEV), F32)], axis=1)
    slots[0] = jnp.concatenate([piece[0:RIM], piece[RIM:]], axis=1)
    for s in range(1, 16):
        slots[s] = slots[0]
    for copy in copies[2:]:
        copy.wait()
    row = [sends[d : d + 1, :].astype(F32) for d in range(4)]
    row.append(jnp.zeros((1, CELLS - GHOSTS), F32))
    row = jnp.concatenate(row, axis=1)
    sel = chosen(row[:, :128])
    copies[1].wait()
    out[0:GHOSTS, :] = exact_dot(sel, fields[...], ((1,), (1,)))
    out[GHOSTS:, 0:CELLS] = jnp.concatenate([named[...].astype(F32), kappa[...], row], axis=0)
    out[GHOSTS:, CELLS:] = jnp.zeros((8, FIELDS - CELLS), F32)


def near_kernel(load, adj, sel, rows, gsel, ksel):
    table = load[GHOSTS:, 0:CELLS]
    named_cells(table, adj, rows, table[6:7, :])
    sel[...] = chosen(table[7:8, :128])
    gsel[...] = lax.dot_general(
        sel[...], adj[CELLS:, :], (((1,), (1,)), ((), ())), preferred_element_type=F32
    ).astype(BF16)
    kappa = jnp.broadcast_to(table[6:7, :], (128, CELLS))
    ksel[...] = exact_dot(sel[...], kappa, ((1,), (1,)), 3)


def gathered(core, slots):
    cells = []
    for m in range(MEM):
        two = slots[core[0] * MEM + m]
        cells += [two, pltpu.roll(two, 64, 1)]
    return jnp.concatenate(cells, axis=0)


def rims_out(rims, outs):
    for d, out in zip(ORDER, outs):
        out[...] = rims[d * RIM : (d + 1) * RIM]


def joined(arrived):
    return jnp.concatenate([arrived[d][...] for d in ORDER], axis=0)


def spread():
    level = lax.broadcasted_iota(jnp.int32, (FIELDS, 128), 0) // MEM
    return (level == lax.broadcasted_iota(jnp.int32, (FIELDS, 128), 1)).astype(F32).astype(BF16)


def first_kernel(core, slots, load, sel, ksel, r0, r1, r2, r3):
    grad = exact_dot(sel[...], gathered(core, slots), ((1,), (0,)), 3)
    lane = lax.broadcasted_iota(jnp.int32, (GHOSTS, 128), 1)
    grad = jnp.where(lane < LEV, grad, 0.0) * ksel[...]
    grad = exact_dot(grad, spread(), ((1,), (1,)), 3)
    rims_out(load[0:GHOSTS, :] * grad, (r0, r1, r2, r3))


def stay(x, adj, rows):
    kappa = rows[0:1, :]
    return x * rows[1:2, :] + exact_dot(kappa * x, adj[0:CELLS, :], ((1,), (0,)))


def stay_out(x, adj, sel, rows, y_out, b_out):
    y = stay(x, adj, rows)
    y_out[...] = y
    b_out[...] = exact_dot(sel[...], rows[0:1, :] * y, ((1,), (1,)))


def first_stay_kernel(core, slots, fields, adj, sel, rows, y_out, b_out, x):
    grad = gathered(core, slots).T
    for l in range(LEV):
        x[l * MEM : (l + 1) * MEM, :] = fields[l * MEM : (l + 1) * MEM, :] * grad[l : l + 1]
    stay_out(x[...], adj, sel, rows, y_out, b_out)


def rim_kernel(b, gsel, ksel, i0, i1, i2, i3, r0, r1, r2, r3, came_out):
    came = joined((i0, i1, i2, i3))
    came_out[...] = came
    rims = b[...] + ksel[:, 0:1] * exact_dot(gsel[...], came, ((1,), (0,)), 3)
    rims_out(rims, (r0, r1, r2, r3))


def arrive(y, ghosts, came):
    return y[...] + exact_dot(came.T, ghosts, ((1,), (0,)))


def stay_kernel(y, adj, sel, rows, came, y_out, b_out):
    x = arrive(y, adj[CELLS:, :], came[...])
    stay_out(x, adj, sel, rows, y_out, b_out)


def dot_split(left, right):
    total = jnp.dot(left[1], right[0], preferred_element_type=F32)
    total = total + jnp.dot(left[0], right[1], preferred_element_type=F32)
    return total + jnp.dot(left[0], right[0], preferred_element_type=F32)


def last_stay_kernel(y, adj, rows, mix_high, mix_low, came, out):
    x = arrive(y, adj[CELLS:, :], came[...])
    out[...] = dot_split((mix_high[...], mix_low[...]), split(stay(x, adj, rows), 2))


def mixed_rims(first, second, back_high, back_low):
    came = jnp.concatenate([first[...], second[...]], axis=0)
    return dot_split(split(came, 2), (back_high[...], back_low[...]))


def near_sides_kernel(y, adj, back_high, back_low, south, north, out):
    rims = mixed_rims(south, north, back_high, back_low)
    out[...] = arrive(y, adj[CELLS + 2 * RIM :, :], rims)


def mix_sides_kernel(back_high, back_low, east, west, east_out, west_out):
    rims = mixed_rims(east, west, back_high, back_low)
    east_out[...] = rims[0:RIM]
    west_out[...] = rims[RIM:]


def home_kernel(vloc, named, mix_high, mix_low, back_high, back_low, ghosts):
    level = lax.broadcasted_iota(jnp.int32, (FIELDS, 128), 0) // MEM
    spread = level == lax.broadcasted_iota(jnp.int32, (FIELDS, 128), 1)
    spread = spread.astype(F32).astype(BF16)[:, 0:LEV]
    row = lax.broadcasted_iota(jnp.int32, (FIELDS, FIELDS), 0) % MEM
    column = lax.broadcasted_iota(jnp.int32, (FIELDS, FIELDS), 1) % MEM
    for square, outs in ((vloc[...].T, (mix_high, mix_low)), (vloc[...], (back_high, back_low))):
        wide = exact_dot(spread, square, ((1,), (0,)), 3)
        full = exact_dot(wide, spread, ((1,), (1,)), 3)
        for out, part in zip(outs, split(jnp.where(row == column, full, 0.0), 2)):
            out[...] = part
    ids = lax.broadcasted_iota(jnp.int32, (2 * RIM, CELLS), 0) + CELLS
    total = jnp.zeros((2 * RIM, CELLS), F32)
    for j in range(6):
        total = total + (ids == named[j : j + 1, :]).astype(F32)
    ghosts[...] = total.astype(BF16)


def last_kernel(count, y, ghosts, east, west, out, held, done):
    alive = lax.broadcasted_iota(jnp.int32, (1, CELLS), 1) < count[0]
    rims = jnp.concatenate([east[...], west[...]], axis=0).T
    copies = []
    for i, first in enumerate(range(0, FIELDS, 112)):
        part = pl.ds(first, min(112, FIELDS - first))
        sides = exact_dot(rims[first : first + 112], ghosts[...], ((1,), (0,)))
        held[part, :] = jnp.where(alive, y[part, :] + sides, 0.0)
        copies.append(pltpu.make_async_copy(held.at[part], out.at[part], done.at[i]))
        copies[-1].start()
    for copy in copies:
        copy.wait()


VM = pl.BlockSpec(memory_space=pltpu.VMEM)
SM = pl.BlockSpec(memory_space=pltpu.SMEM)


def call(kernel, shapes, args, scalars=0, flops=10**8, scratch=(), rest=VM, vmem=32, outs=None):
    specs = [SM] * scalars + [rest] * (len(args) - scalars)
    return pl.pallas_call(
        kernel,
        out_shape=[jax.ShapeDtypeStruct(s, t) for s, t in shapes],
        in_specs=specs,
        out_specs=[outs or VM] * len(shapes),
        scratch_shapes=list(scratch),
        cost_estimate=pl.CostEstimate(flops=flops, bytes_accessed=10**6, transcendentals=0),
        compiler_params=pltpu.CompilerParams(vmem_limit_bytes=vmem * 1024 * 1024),
    )(*args)


def exchange(rims):
    return [lax.ppermute(rim, AXES, route) for rim, route in zip(rims, ROUTES)]


def local(perturbations, gradient, kappa, vloc, neighbors, send_lists, counts):
    fields = perturbations.transpose(1, 0, 2).reshape(FIELDS, CELLS)
    state = ((FIELDS, CELLS), F32)
    border = ((GHOSTS, FIELDS), F32)
    rim_shapes = [((RIM, FIELDS), F32)] * 4
    core = (lax.axis_index("member") % 2).reshape(1)
    slots, load = call(
        pack_kernel,
        [((16, RIM, 128), F32), ((GHOSTS + 8, FIELDS), F32)],
        (
            gradient.reshape(LEV, 32).T,
            fields,
            kappa.reshape(1, CELLS),
            neighbors,
            send_lists,
        ),
        scratch=[
            pltpu.VMEM((32, LEV), F32),
            pltpu.VMEM((FIELDS, CELLS), F32),
            pltpu.VMEM((1, CELLS), F32),
            pltpu.VMEM((6, CELLS), jnp.int32),
            pltpu.VMEM((4, RIM), jnp.int32),
            pltpu.SemaphoreType.DMA((5,)),
        ],
        rest=pl.BlockSpec(memory_space=pltpu.HBM),
        vmem=60,
    )
    load = lax.ppermute(load, AXES, GO)
    load, fields = lax.optimization_barrier((load, fields))
    fields = lax.ppermute(fields, AXES, GO)
    slots = lax.all_to_all(slots, ("yh", "member"), 0, 0)
    adj, sel, rows, gsel, ksel = call(
        near_kernel,
        [
            ((NULL, CELLS), BF16),
            ((GHOSTS, CELLS), BF16),
            ((8, CELLS), F32),
            ((GHOSTS, GHOSTS), BF16),
            ((GHOSTS, 128), F32),
        ],
        (load,),
        flops=10**10,
    )
    gsel, vloc = lax.optimization_barrier((gsel, vloc))
    square = ((FIELDS, FIELDS), BF16)
    mix_high, mix_low, back_high, back_low, ghosts = call(
        home_kernel, [square] * 4 + [((2 * RIM, CELLS), BF16)], (vloc, neighbors)
    )
    sel, ghosts = lax.optimization_barrier((sel, ghosts))
    rims = call(
        first_kernel, rim_shapes, (core, slots, load, sel, ksel), scalars=1, flops=2*10**10
    )
    came = exchange(rims)
    y, b = call(
        first_stay_kernel,
        [state, border],
        (core, slots, fields, adj, sel, rows),
        scalars=1,
        scratch=[pltpu.VMEM((FIELDS, CELLS), F32)],
    )
    for step in range(1, STEPS - 1):
        *rims, came = call(rim_kernel, rim_shapes + [border], (b, gsel, ksel, *came))
        y, b = call(stay_kernel, [state, border], (y, adj, sel, rows, came))
        came = exchange(rims)
    east, south, west, north, came = call(
        rim_kernel, rim_shapes + [border], (b, gsel, ksel, *came)
    )
    (y,) = call(last_stay_kernel, [state], (y, adj, rows, mix_high, mix_low, came))
    south = lax.ppermute(south, AXES, SOUTH)
    north = lax.ppermute(north, AXES, NORTH)
    east, west = call(mix_sides_kernel, rim_shapes[:2], (back_high, back_low, east, west))
    (y,) = call(near_sides_kernel, [state], (y, adj, back_high, back_low, south, north))
    y, east, west = lax.optimization_barrier((y, east, west))
    y = lax.ppermute(y, AXES, BACK)
    east = lax.ppermute(east, AXES, homeward(EAST))
    west = lax.ppermute(west, AXES, homeward(WEST))
    (out,) = call(
        last_kernel,
        [state],
        (counts, y, ghosts, east, west),
        scalars=1,
        scratch=[pltpu.VMEM((FIELDS, CELLS), F32), pltpu.SemaphoreType.DMA((4,))],
        outs=pl.BlockSpec(memory_space=pltpu.HBM),
    )
    return out.reshape(LEV, MEM, CELLS).transpose(1, 0, 2)


def solution(mesh):
    parts = Mesh(mesh.devices.reshape(8, 4, 2, 8), AXES)
    patch = ("x", "yh", "z")
    return jax.shard_map(
        local,
        mesh=parts,
        in_specs=(
            P("member", None, patch),
            P(None, patch, "member"),
            P(patch),
            P(),
            P(None, patch),
            P(None, patch),
            P(patch),
        ),
        out_specs=P("member", None, patch),
        check_vma=False,
    )
```

```python
import itertools

import jax
import jax.numpy as jnp
from jax import lax
from jax.experimental import pallas as pl
from jax.experimental.pallas import tpu as pltpu
from jax.sharding import Mesh
from jax.sharding import PartitionSpec as P

STEPS = 4
AXES = ("member", "x", "yh", "z")
LEV = 55
MEM = 8
FIELDS = LEV * MEM
CELLS = 256
RIM = 16
GHOSTS = 4 * RIM
NULL = CELLS + GHOSTS
F32 = jnp.float32
BF16 = jnp.bfloat16


def flat(x, yh, l, z, core):
    return (l * 2 + core) * 64 + (x % 4) * 16 + yh * 8 + z % 8


def pairs(move):
    every = itertools.product(range(4), range(2), range(4), range(8), range(2))
    return sorted((flat(*c), flat(*move(*c))) for c in every)


def next_column(x, yh, l, z, core):
    if z < 7:
        return x, yh, l, z + 1, core
    return x + core, yh, l, 0, 1 - core


def near(x, yh, l, z, core):
    y = (l + 2 + 4 * core) % 8
    return x, y // 4, y % 4, z, yh


GO = pairs(near)
BACK = sorted((b, a) for a, b in GO)
EAST = pairs(next_column)
WEST = sorted((b, a) for a, b in EAST)
SOUTH = pairs(lambda x, yh, l, z, core: (x + core, yh, l, z, 1 - core))
NORTH = sorted((b, a) for a, b in SOUTH)
ROUTES = (SOUTH, EAST, WEST, NORTH)
ORDER = (2, 0, 1, 3)
PLACE = (1, 2, 0, 3)
HOME = dict(BACK)


def homeward(route):
    return [(a, HOME[b]) for a, b in route]


def split(value, count):
    parts = []
    for _ in range(count):
        parts.append(value.astype(BF16))
        value = value - parts[-1].astype(F32)
    return parts


def exact_dot(left, right, dims, count=2):
    split_left = left.dtype == F32
    total = None
    for part in reversed(split(left if split_left else right, count)):
        a, b = (part, right) if split_left else (left, part)
        term = lax.dot_general(a, b, (dims, ((), ())), preferred_element_type=F32)
        total = term if total is None else total + term
    return total


def chosen(sends):
    column = jnp.broadcast_to(sends, (128, 128)).T[0:GHOSTS].astype(jnp.int32)
    slots = lax.broadcasted_iota(jnp.int32, (GHOSTS, CELLS), 1)
    return (jnp.concatenate([column, column], axis=1) == slots).astype(F32).astype(BF16)


def named_cells(table, adj, rows, kappa):
    ids = lax.broadcasted_iota(jnp.int32, (NULL, CELLS), 0)
    total = jnp.zeros((NULL, CELLS), F32)
    degree = jnp.zeros((1, CELLS), F32)
    for j in range(6):
        named = table[j : j + 1, :].astype(jnp.int32)
        total = total + (ids == named).astype(F32)
        degree = degree + (named < NULL).astype(F32)
    adj[...] = total.astype(BF16)
    rows[...] = jnp.concatenate(
        [kappa, 1.0 - degree * kappa, jnp.zeros((6, CELLS), F32)], axis=0
    )


def pack_kernel(grad_in, fields_in, kappa_in, named_in, sends_in, slots, out, *scratch):
    *held, done = scratch
    given = (grad_in, fields_in, kappa_in, named_in, sends_in)
    copies = [
        pltpu.make_async_copy(here, there, done.at[i])
        for i, (here, there) in enumerate(zip(given, held))
    ]
    for copy in copies:
        copy.start()
    for copy in copies:
        copy.wait()
    grad, fields, kappa, named, sends = held
    piece = jnp.concatenate([grad[...], jnp.zeros((32, 64 - LEV), F32)], axis=1)
    slots[0] = jnp.concatenate([piece[0:RIM], piece[RIM:]], axis=1)
    for s in range(1, 16):
        slots[s] = slots[0]
    row = [sends[d : d + 1, :].astype(F32) for d in range(4)]
    row.append(jnp.zeros((1, CELLS - GHOSTS), F32))
    row = jnp.concatenate(row, axis=1)
    out[0:GHOSTS, :] = exact_dot(chosen(row[:, :128]), fields[...], ((1,), (1,)), 3)
    out[GHOSTS:, 0:CELLS] = jnp.concatenate([named[...].astype(F32), kappa[...], row], axis=0)
    out[GHOSTS:, CELLS:] = jnp.zeros((8, FIELDS - CELLS), F32)


def near_kernel(load, adj, sel, rows, gsel, ksel):
    table = load[GHOSTS:, 0:CELLS]
    named_cells(table, adj, rows, table[6:7, :])
    sel[...] = chosen(table[7:8, :128])
    gsel[...] = lax.dot_general(
        sel[...], adj[CELLS:, :], (((1,), (1,)), ((), ())), preferred_element_type=F32
    ).astype(BF16)
    kappa = jnp.broadcast_to(table[6:7, :], (128, CELLS))
    ksel[...] = exact_dot(sel[...], kappa, ((1,), (1,)), 3)


def gathered(core, slots):
    cells = []
    for m in range(MEM):
        two = slots[core[0] * MEM + m]
        cells += [two, pltpu.roll(two, 64, 1)]
    return jnp.concatenate(cells, axis=0)


def rims_out(rims, outs):
    for d, out in zip(ORDER, outs):
        out[...] = rims[d * RIM : (d + 1) * RIM]


def joined(arrived):
    return jnp.concatenate([arrived[d][...] for d in PLACE], axis=0)


def spread():
    level = lax.broadcasted_iota(jnp.int32, (FIELDS, 128), 0) // MEM
    return (level == lax.broadcasted_iota(jnp.int32, (FIELDS, 128), 1)).astype(F32).astype(BF16)


def first_kernel(core, slots, load, sel, ksel, r0, r1, r2, r3):
    grad = exact_dot(sel[...], gathered(core, slots), ((1,), (0,)), 3)
    lane = lax.broadcasted_iota(jnp.int32, (GHOSTS, 128), 1)
    grad = jnp.where(lane < LEV, grad, 0.0) * ksel[...]
    grad = exact_dot(grad, spread(), ((1,), (1,)), 3)
    rims_out(load[0:GHOSTS, :] * grad, (r0, r1, r2, r3))


def stay(x, adj, rows):
    kappa = rows[0:1, :]
    return x * rows[1:2, :] + exact_dot(kappa * x, adj[0:CELLS, :], ((1,), (0,)))


def stay_out(x, adj, sel, rows, y_out, b_out):
    y = stay(x, adj, rows)
    y_out[...] = y
    b_out[...] = exact_dot(sel[...], rows[0:1, :] * y, ((1,), (1,)))


def first_stay_kernel(core, slots, fields, adj, sel, rows, y_out, b_out, x):
    grad = gathered(core, slots).T
    for l in range(LEV):
        x[l * MEM : (l + 1) * MEM, :] = fields[l * MEM : (l + 1) * MEM, :] * grad[l : l + 1]
    stay_out(x[...], adj, sel, rows, y_out, b_out)


def rim_kernel(b, gsel, ksel, i0, i1, i2, i3, r0, r1, r2, r3, came_out):
    came = joined((i0, i1, i2, i3))
    came_out[...] = came
    rims = b[...] + ksel[:, 0:1] * exact_dot(gsel[...], came, ((1,), (0,)), 3)
    rims_out(rims, (r0, r1, r2, r3))


def arrive(y, ghosts, came):
    return y[...] + exact_dot(came.T, ghosts, ((1,), (0,)))


def stay_kernel(y, adj, sel, rows, came, y_out, b_out):
    x = arrive(y, adj[CELLS:, :], came[...])
    stay_out(x, adj, sel, rows, y_out, b_out)


def dot_split(left, right):
    total = jnp.dot(left[1], right[0], preferred_element_type=F32)
    total = total + jnp.dot(left[0], right[1], preferred_element_type=F32)
    return total + jnp.dot(left[0], right[0], preferred_element_type=F32)


def last_stay_kernel(y, adj, rows, mix_high, mix_low, came, out):
    x = arrive(y, adj[CELLS:, :], came[...])
    out[...] = dot_split((mix_high[...], mix_low[...]), split(stay(x, adj, rows), 2))


def mixed_rims(first, second, back_high, back_low):
    came = jnp.concatenate([first[...], second[...]], axis=0)
    return dot_split(split(came, 2), (back_high[...], back_low[...]))


def near_sides_kernel(y, adj, back_high, back_low, south, north, out):
    rims = mixed_rims(south, north, back_high, back_low)
    out[...] = arrive(y, adj[CELLS + 2 * RIM :, :], rims)


def mix_sides_kernel(back_high, back_low, east, west, east_out, west_out):
    rims = mixed_rims(east, west, back_high, back_low)
    east_out[...] = rims[0:RIM]
    west_out[...] = rims[RIM:]


def home_kernel(vloc, named, mix_high, mix_low, back_high, back_low, ghosts):
    level = lax.broadcasted_iota(jnp.int32, (FIELDS, 128), 0) // MEM
    spread = level == lax.broadcasted_iota(jnp.int32, (FIELDS, 128), 1)
    spread = spread.astype(F32).astype(BF16)[:, 0:LEV]
    row = lax.broadcasted_iota(jnp.int32, (FIELDS, FIELDS), 0) % MEM
    column = lax.broadcasted_iota(jnp.int32, (FIELDS, FIELDS), 1) % MEM
    for square, outs in ((vloc[...].T, (mix_high, mix_low)), (vloc[...], (back_high, back_low))):
        wide = exact_dot(spread, square, ((1,), (0,)), 3)
        full = exact_dot(wide, spread, ((1,), (1,)), 3)
        for out, part in zip(outs, split(jnp.where(row == column, full, 0.0), 2)):
            out[...] = part
    ids = lax.broadcasted_iota(jnp.int32, (2 * RIM, CELLS), 0) + CELLS
    total = jnp.zeros((2 * RIM, CELLS), F32)
    for j in range(6):
        total = total + (ids == named[j : j + 1, :]).astype(F32)
    ghosts[...] = total.astype(BF16)


def last_kernel(count, y, ghosts, east, west, out):
    alive = lax.broadcasted_iota(jnp.int32, (1, CELLS), 1) < count[0]
    rims = jnp.concatenate([east[...], west[...]], axis=0)
    out[...] = jnp.where(alive, arrive(y, ghosts[...], rims), 0.0)


VM = pl.BlockSpec(memory_space=pltpu.VMEM)
SM = pl.BlockSpec(memory_space=pltpu.SMEM)


def call(kernel, shapes, args, scalars=0, flops=10**8, scratch=(), rest=VM, vmem=32):
    specs = [SM] * scalars + [rest] * (len(args) - scalars)
    return pl.pallas_call(
        kernel,
        out_shape=[jax.ShapeDtypeStruct(s, t) for s, t in shapes],
        in_specs=specs,
        out_specs=[VM] * len(shapes),
        scratch_shapes=list(scratch),
        cost_estimate=pl.CostEstimate(flops=flops, bytes_accessed=10**6, transcendentals=0),
        compiler_params=pltpu.CompilerParams(vmem_limit_bytes=vmem * 1024 * 1024),
    )(*args)


def exchange(rims):
    return [lax.ppermute(rim, AXES, route) for rim, route in zip(rims, ROUTES)]


def local(perturbations, gradient, kappa, vloc, neighbors, send_lists, counts):
    fields = perturbations.transpose(1, 0, 2).reshape(FIELDS, CELLS)
    state = ((FIELDS, CELLS), F32)
    border = ((GHOSTS, FIELDS), F32)
    rim_shapes = [((RIM, FIELDS), F32)] * 4
    core = (lax.axis_index("member") % 2).reshape(1)
    slots, load = call(
        pack_kernel,
        [((16, RIM, 128), F32), ((GHOSTS + 8, FIELDS), F32)],
        (
            gradient.reshape(LEV, 32).T,
            fields,
            kappa.reshape(1, CELLS),
            neighbors,
            send_lists,
        ),
        scratch=[
            pltpu.VMEM((32, LEV), F32),
            pltpu.VMEM((FIELDS, CELLS), F32),
            pltpu.VMEM((1, CELLS), F32),
            pltpu.VMEM((6, CELLS), jnp.int32),
            pltpu.VMEM((4, RIM), jnp.int32),
            pltpu.SemaphoreType.DMA((5,)),
        ],
        rest=pl.BlockSpec(memory_space=pltpu.HBM),
        vmem=60,
    )
    load = lax.ppermute(load, AXES, GO)
    load, fields = lax.optimization_barrier((load, fields))
    fields = lax.ppermute(fields, AXES, GO)
    slots = lax.all_to_all(slots, ("yh", "member"), 0, 0)
    adj, sel, rows, gsel, ksel = call(
        near_kernel,
        [
            ((NULL, CELLS), BF16),
            ((GHOSTS, CELLS), BF16),
            ((8, CELLS), F32),
            ((GHOSTS, GHOSTS), BF16),
            ((GHOSTS, 128), F32),
        ],
        (load,),
        flops=10**10,
    )
    gsel, vloc = lax.optimization_barrier((gsel, vloc))
    square = ((FIELDS, FIELDS), BF16)
    mix_high, mix_low, back_high, back_low, ghosts = call(
        home_kernel, [square] * 4 + [((2 * RIM, CELLS), BF16)], (vloc, neighbors)
    )
    sel, ghosts = lax.optimization_barrier((sel, ghosts))
    rims = call(
        first_kernel, rim_shapes, (core, slots, load, sel, ksel), scalars=1, flops=2*10**10
    )
    came = exchange(rims)
    y, b = call(
        first_stay_kernel,
        [state, border],
        (core, slots, fields, adj, sel, rows),
        scalars=1,
        scratch=[pltpu.VMEM((FIELDS, CELLS), F32)],
    )
    for step in range(1, STEPS - 1):
        *rims, came = call(rim_kernel, rim_shapes + [border], (b, gsel, ksel, *came))
        y, b = call(stay_kernel, [state, border], (y, adj, sel, rows, came))
        came = exchange(rims)
    south, east, west, north, came = call(
        rim_kernel, rim_shapes + [border], (b, gsel, ksel, *came)
    )
    (y,) = call(last_stay_kernel, [state], (y, adj, rows, mix_high, mix_low, came))
    south = lax.ppermute(south, AXES, SOUTH)
    north = lax.ppermute(north, AXES, NORTH)
    east, west = call(mix_sides_kernel, rim_shapes[:2], (back_high, back_low, east, west))
    (y,) = call(near_sides_kernel, [state], (y, adj, back_high, back_low, south, north))
    y, east, west = lax.optimization_barrier((y, east, west))
    y = lax.ppermute(y, AXES, BACK)
    east = lax.ppermute(east, AXES, homeward(EAST))
    west = lax.ppermute(west, AXES, homeward(WEST))
    (out,) = call(last_kernel, [state], (counts, y, ghosts, east, west), scalars=1)
    return out.reshape(LEV, MEM, CELLS).transpose(1, 0, 2)


def solution(mesh):
    parts = Mesh(mesh.devices.reshape(8, 4, 2, 8), AXES)
    patch = ("x", "yh", "z")
    return jax.shard_map(
        local,
        mesh=parts,
        in_specs=(
            P("member", None, patch),
            P(None, patch, "member"),
            P(patch),
            P(),
            P(None, patch),
            P(None, patch),
            P(patch),
        ),
        out_specs=P("member", None, patch),
        check_vma=False,
    )
```

```python
import itertools

import jax
import jax.numpy as jnp
from jax import lax
from jax.experimental import pallas as pl
from jax.experimental.pallas import tpu as pltpu
from jax.sharding import Mesh
from jax.sharding import PartitionSpec as P

STEPS = 4
AXES = ("member", "x", "yh", "z")
LEV = 55
MEM = 8
FIELDS = LEV * MEM
CELLS = 256
RIM = 16
GHOSTS = 4 * RIM
NULL = CELLS + GHOSTS
F32 = jnp.float32
BF16 = jnp.bfloat16


def flat(x, yh, l, z, core):
    return (l * 2 + core) * 64 + (x % 4) * 16 + yh * 8 + z % 8


def pairs(move):
    every = itertools.product(range(4), range(2), range(4), range(8), range(2))
    return sorted((flat(*c), flat(*move(*c))) for c in every)


def next_column(x, yh, l, z, core):
    if z < 7:
        return x, yh, l, z + 1, core
    return x + core, yh, l, 0, 1 - core


def near(x, yh, l, z, core):
    y = (l + 2 + 4 * core) % 8
    return x, y // 4, y % 4, z, yh


GO = pairs(near)
BACK = sorted((b, a) for a, b in GO)
EAST = pairs(next_column)
WEST = sorted((b, a) for a, b in EAST)
SOUTH = pairs(lambda x, yh, l, z, core: (x + core, yh, l, z, 1 - core))
NORTH = sorted((b, a) for a, b in SOUTH)
ROUTES = (SOUTH, EAST, WEST, NORTH)
ORDER = (2, 0, 1, 3)
PLACE = (1, 2, 0, 3)
HOME = dict(BACK)


def homeward(route):
    return [(a, HOME[b]) for a, b in route]


def split(value, count):
    parts = []
    for _ in range(count):
        parts.append(value.astype(BF16))
        value = value - parts[-1].astype(F32)
    return parts


def exact_dot(left, right, dims, count=2):
    split_left = left.dtype == F32
    total = None
    for part in reversed(split(left if split_left else right, count)):
        a, b = (part, right) if split_left else (left, part)
        term = lax.dot_general(a, b, (dims, ((), ())), preferred_element_type=F32)
        total = term if total is None else total + term
    return total


def chosen(sends):
    column = jnp.broadcast_to(sends, (128, 128)).T[0:GHOSTS].astype(jnp.int32)
    slots = lax.broadcasted_iota(jnp.int32, (GHOSTS, CELLS), 1)
    return (jnp.concatenate([column, column], axis=1) == slots).astype(F32).astype(BF16)


def named_cells(table, adj, rows, kappa):
    ids = lax.broadcasted_iota(jnp.int32, (NULL, CELLS), 0)
    total = jnp.zeros((NULL, CELLS), F32)
    degree = jnp.zeros((1, CELLS), F32)
    for j in range(6):
        named = table[j : j + 1, :].astype(jnp.int32)
        total = total + (ids == named).astype(F32)
        degree = degree + (named < NULL).astype(F32)
    adj[...] = total.astype(BF16)
    rows[...] = jnp.concatenate(
        [kappa, 1.0 - degree * kappa, jnp.zeros((6, CELLS), F32)], axis=0
    )


def pack_kernel(grad_in, fields_in, kappa_in, named_in, sends_in, slots, out, *scratch):
    *held, done = scratch
    given = (grad_in, fields_in, kappa_in, named_in, sends_in)
    copies = [
        pltpu.make_async_copy(here, there, done.at[i])
        for i, (here, there) in enumerate(zip(given, held))
    ]
    for copy in copies:
        copy.start()
    grad, fields, kappa, named, sends = held
    copies[0].wait()
    piece = jnp.concatenate([grad[...], jnp.zeros((32, 64 - LEV), F32)], axis=1)
    slots[0] = jnp.concatenate([piece[0:RIM], piece[RIM:]], axis=1)
    for s in range(1, 16):
        slots[s] = slots[0]
    for copy in copies[2:]:
        copy.wait()
    row = [sends[d : d + 1, :].astype(F32) for d in range(4)]
    row.append(jnp.zeros((1, CELLS - GHOSTS), F32))
    row = jnp.concatenate(row, axis=1)
    sel = chosen(row[:, :128])
    copies[1].wait()
    out[0:GHOSTS, :] = exact_dot(sel, fields[...], ((1,), (1,)))
    out[GHOSTS:, 0:CELLS] = jnp.concatenate([named[...].astype(F32), kappa[...], row], axis=0)
    out[GHOSTS:, CELLS:] = jnp.zeros((8, FIELDS - CELLS), F32)


def near_kernel(load, adj, sel, rows, gsel, ksel):
    table = load[GHOSTS:, 0:CELLS]
    named_cells(table, adj, rows, table[6:7, :])
    sel[...] = chosen(table[7:8, :128])
    gsel[...] = lax.dot_general(
        sel[...], adj[CELLS:, :], (((1,), (1,)), ((), ())), preferred_element_type=F32
    ).astype(BF16)
    kappa = jnp.broadcast_to(table[6:7, :], (128, CELLS))
    ksel[...] = exact_dot(sel[...], kappa, ((1,), (1,)), 3)


def gathered(core, slots):
    cells = []
    for m in range(MEM):
        two = slots[core[0] * MEM + m]
        cells += [two, pltpu.roll(two, 64, 1)]
    return jnp.concatenate(cells, axis=0)


def rims_out(rims, outs):
    for d, out in zip(ORDER, outs):
        out[...] = rims[d * RIM : (d + 1) * RIM]


def joined(arrived):
    return jnp.concatenate([arrived[d][...] for d in PLACE], axis=0)


def spread():
    level = lax.broadcasted_iota(jnp.int32, (FIELDS, 128), 0) // MEM
    return (level == lax.broadcasted_iota(jnp.int32, (FIELDS, 128), 1)).astype(F32).astype(BF16)


def first_kernel(core, slots, load, sel, ksel, r0, r1, r2, r3):
    grad = exact_dot(sel[...], gathered(core, slots), ((1,), (0,)), 3)
    lane = lax.broadcasted_iota(jnp.int32, (GHOSTS, 128), 1)
    grad = jnp.where(lane < LEV, grad, 0.0) * ksel[...]
    grad = exact_dot(grad, spread(), ((1,), (1,)), 3)
    rims_out(load[0:GHOSTS, :] * grad, (r0, r1, r2, r3))


def stay(x, adj, rows):
    kappa = rows[0:1, :]
    return x * rows[1:2, :] + exact_dot(kappa * x, adj[0:CELLS, :], ((1,), (0,)))


def stay_out(x, adj, sel, rows, y_out, b_out):
    y = stay(x, adj, rows)
    y_out[...] = y
    b_out[...] = exact_dot(sel[...], rows[0:1, :] * y, ((1,), (1,)))


def first_stay_kernel(core, slots, fields, adj, sel, rows, y_out, b_out, x):
    grad = gathered(core, slots).T
    for l in range(LEV):
        x[l * MEM : (l + 1) * MEM, :] = fields[l * MEM : (l + 1) * MEM, :] * grad[l : l + 1]
    stay_out(x[...], adj, sel, rows, y_out, b_out)


def rim_kernel(b, gsel, ksel, i0, i1, i2, i3, r0, r1, r2, r3, came_out):
    came = joined((i0, i1, i2, i3))
    came_out[...] = came
    rims = b[...] + ksel[:, 0:1] * exact_dot(gsel[...], came, ((1,), (0,)), 3)
    rims_out(rims, (r0, r1, r2, r3))


def arrive(y, ghosts, came):
    return y[...] + exact_dot(came.T, ghosts, ((1,), (0,)))


def stay_kernel(y, adj, sel, rows, came, y_out, b_out):
    x = arrive(y, adj[CELLS:, :], came[...])
    stay_out(x, adj, sel, rows, y_out, b_out)


def dot_split(left, right):
    total = jnp.dot(left[1], right[0], preferred_element_type=F32)
    total = total + jnp.dot(left[0], right[1], preferred_element_type=F32)
    return total + jnp.dot(left[0], right[0], preferred_element_type=F32)


def last_stay_kernel(y, adj, rows, mix_high, mix_low, came, out):
    x = arrive(y, adj[CELLS:, :], came[...])
    out[...] = dot_split((mix_high[...], mix_low[...]), split(stay(x, adj, rows), 2))


def mixed_rims(first, second, back_high, back_low):
    came = jnp.concatenate([first[...], second[...]], axis=0)
    return dot_split(split(came, 2), (back_high[...], back_low[...]))


def near_sides_kernel(y, adj, back_high, back_low, south, north, out):
    rims = mixed_rims(south, north, back_high, back_low)
    out[...] = arrive(y, adj[CELLS + 2 * RIM :, :], rims)


def mix_sides_kernel(back_high, back_low, east, west, east_out, west_out):
    rims = mixed_rims(east, west, back_high, back_low)
    east_out[...] = rims[0:RIM]
    west_out[...] = rims[RIM:]


def home_kernel(vloc, named, mix_high, mix_low, back_high, back_low, ghosts):
    level = lax.broadcasted_iota(jnp.int32, (FIELDS, 128), 0) // MEM
    spread = level == lax.broadcasted_iota(jnp.int32, (FIELDS, 128), 1)
    spread = spread.astype(F32).astype(BF16)[:, 0:LEV]
    row = lax.broadcasted_iota(jnp.int32, (FIELDS, FIELDS), 0) % MEM
    column = lax.broadcasted_iota(jnp.int32, (FIELDS, FIELDS), 1) % MEM
    for square, outs in ((vloc[...].T, (mix_high, mix_low)), (vloc[...], (back_high, back_low))):
        wide = exact_dot(spread, square, ((1,), (0,)), 3)
        full = exact_dot(wide, spread, ((1,), (1,)), 3)
        for out, part in zip(outs, split(jnp.where(row == column, full, 0.0), 2)):
            out[...] = part
    ids = lax.broadcasted_iota(jnp.int32, (2 * RIM, CELLS), 0) + CELLS
    total = jnp.zeros((2 * RIM, CELLS), F32)
    for j in range(6):
        total = total + (ids == named[j : j + 1, :]).astype(F32)
    ghosts[...] = total.astype(BF16)


def last_kernel(count, y, ghosts, east, west, out, held, done):
    alive = lax.broadcasted_iota(jnp.int32, (1, CELLS), 1) < count[0]
    rims = jnp.concatenate([east[...], west[...]], axis=0).T
    copies = []
    for i, first in enumerate(range(0, FIELDS, 112)):
        part = pl.ds(first, min(112, FIELDS - first))
        sides = exact_dot(rims[first : first + 112], ghosts[...], ((1,), (0,)))
        held[part, :] = jnp.where(alive, y[part, :] + sides, 0.0)
        copies.append(pltpu.make_async_copy(held.at[part], out.at[part], done.at[i]))
        copies[-1].start()
    for copy in copies:
        copy.wait()


VM = pl.BlockSpec(memory_space=pltpu.VMEM)
SM = pl.BlockSpec(memory_space=pltpu.SMEM)


def call(kernel, shapes, args, scalars=0, flops=10**8, scratch=(), rest=VM, vmem=32, outs=None):
    specs = [SM] * scalars + [rest] * (len(args) - scalars)
    return pl.pallas_call(
        kernel,
        out_shape=[jax.ShapeDtypeStruct(s, t) for s, t in shapes],
        in_specs=specs,
        out_specs=[outs or VM] * len(shapes),
        scratch_shapes=list(scratch),
        cost_estimate=pl.CostEstimate(flops=flops, bytes_accessed=10**6, transcendentals=0),
        compiler_params=pltpu.CompilerParams(vmem_limit_bytes=vmem * 1024 * 1024),
    )(*args)


def exchange(rims):
    return [lax.ppermute(rim, AXES, route) for rim, route in zip(rims, ROUTES)]


def local(perturbations, gradient, kappa, vloc, neighbors, send_lists, counts):
    fields = perturbations.transpose(1, 0, 2).reshape(FIELDS, CELLS)
    state = ((FIELDS, CELLS), F32)
    border = ((GHOSTS, FIELDS), F32)
    rim_shapes = [((RIM, FIELDS), F32)] * 4
    core = (lax.axis_index("member") % 2).reshape(1)
    slots, load = call(
        pack_kernel,
        [((16, RIM, 128), F32), ((GHOSTS + 8, FIELDS), F32)],
        (
            gradient.reshape(LEV, 32).T,
            fields,
            kappa.reshape(1, CELLS),
            neighbors,
            send_lists,
        ),
        scratch=[
            pltpu.VMEM((32, LEV), F32),
            pltpu.VMEM((FIELDS, CELLS), F32),
            pltpu.VMEM((1, CELLS), F32),
            pltpu.VMEM((6, CELLS), jnp.int32),
            pltpu.VMEM((4, RIM), jnp.int32),
            pltpu.SemaphoreType.DMA((5,)),
        ],
        rest=pl.BlockSpec(memory_space=pltpu.HBM),
        vmem=60,
    )
    load = lax.ppermute(load, AXES, GO)
    load, fields = lax.optimization_barrier((load, fields))
    fields = lax.ppermute(fields, AXES, GO)
    slots = lax.all_to_all(slots, ("yh", "member"), 0, 0)
    adj, sel, rows, gsel, ksel = call(
        near_kernel,
        [
            ((NULL, CELLS), BF16),
            ((GHOSTS, CELLS), BF16),
            ((8, CELLS), F32),
            ((GHOSTS, GHOSTS), BF16),
            ((GHOSTS, 128), F32),
        ],
        (load,),
        flops=10**10,
    )
    gsel, vloc = lax.optimization_barrier((gsel, vloc))
    square = ((FIELDS, FIELDS), BF16)
    mix_high, mix_low, back_high, back_low, ghosts = call(
        home_kernel, [square] * 4 + [((2 * RIM, CELLS), BF16)], (vloc, neighbors)
    )
    sel, ghosts = lax.optimization_barrier((sel, ghosts))
    rims = call(
        first_kernel, rim_shapes, (core, slots, load, sel, ksel), scalars=1, flops=2*10**10
    )
    came = exchange(rims)
    y, b = call(
        first_stay_kernel,
        [state, border],
        (core, slots, fields, adj, sel, rows),
        scalars=1,
        scratch=[pltpu.VMEM((FIELDS, CELLS), F32)],
    )
    for step in range(1, STEPS - 1):
        *rims, came = call(rim_kernel, rim_shapes + [border], (b, gsel, ksel, *came))
        y, b = call(stay_kernel, [state, border], (y, adj, sel, rows, came))
        came = exchange(rims)
    south, east, west, north, came = call(
        rim_kernel, rim_shapes + [border], (b, gsel, ksel, *came)
    )
    (y,) = call(last_stay_kernel, [state], (y, adj, rows, mix_high, mix_low, came))
    south = lax.ppermute(south, AXES, SOUTH)
    north = lax.ppermute(north, AXES, NORTH)
    east, west = call(mix_sides_kernel, rim_shapes[:2], (back_high, back_low, east, west))
    (y,) = call(near_sides_kernel, [state], (y, adj, back_high, back_low, south, north))
    y, east, west = lax.optimization_barrier((y, east, west))
    y = lax.ppermute(y, AXES, BACK)
    east = lax.ppermute(east, AXES, homeward(EAST))
    west = lax.ppermute(west, AXES, homeward(WEST))
    (out,) = call(
        last_kernel,
        [state],
        (counts, y, ghosts, east, west),
        scalars=1,
        scratch=[pltpu.VMEM((FIELDS, CELLS), F32), pltpu.SemaphoreType.DMA((4,))],
        outs=pl.BlockSpec(memory_space=pltpu.HBM),
    )
    return out.reshape(LEV, MEM, CELLS).transpose(1, 0, 2)


def solution(mesh):
    parts = Mesh(mesh.devices.reshape(8, 4, 2, 8), AXES)
    patch = ("x", "yh", "z")
    return jax.shard_map(
        local,
        mesh=parts,
        in_specs=(
            P("member", None, patch),
            P(None, patch, "member"),
            P(patch),
            P(),
            P(None, patch),
            P(None, patch),
            P(patch),
        ),
        out_specs=P("member", None, patch),
        check_vma=False,
    )
```
